32 devices in a mesh: depth: 8 (over y, x, core), strip: 4 (over z).
Axes of the slice: x: 2, y: 2, z: 4, core: 2. Of those that a mesh axis runs over, the one named last changes fastest.
Arguments:
- density: float32 [32, 64, 2048], P('depth', 'strip'), may hold values from -6 to 6
- materials: int32 [32, 64, 2048], P('depth', 'strip'), may hold values from 0 to 3
- occupancy_flags: int32 [8, 4, 16], P('depth', 'strip'), may hold values from 0 to 1, as said below
- tf_color: float32 [4, 3, 16], replicated, may hold values from 0.1 to 1
- tf_opacity: float32 [4, 16], replicated, may hold values from 0.0005 to 0.05
Outputs:
- image: float32 [4, 64, 2048], P(None, 'strip', 'depth')
The draws below stay inside these ranges and needn't reach their ends.
Inputs may be any that keep to these rules, and one draw needn't show every extreme that they name: `occupancy_flags`: occupied tiles cluster around one depth slab drawn from the seed; the share of occupied tiles differs strongly between depth slabs.
All inputs are finite; a program needn't handle non-finite values.
Results may differ from the reference program's by a relative error of at most 0.0003.
Values sent between devices are 32-bit elements; how exact they have to be, the bound alone decides.
No kernel may reach another device: no remote copies, remote signals or barrier semaphores. Data moves between devices by JAX's collectives and lax.ppermute only.
A program may use at most 64 MiB of HBM per device.

```python
import math
import jax
import jax.numpy as jnp
from jax import lax

DZ = 4
RY = 16
COLS = 2048
KNOTS = 16
MATS = 4
TILES = 16
NZ = 32
NY = 64
N_DEPTH = 8
N_STRIP = 4


def draw_occupancy_flags(key, part):
    key_centre = jax.random.fold_in(key, 11)
    key_rolls = jax.random.fold_in(key, 23)
    centre = jax.random.randint(key_centre, (), 0, N_DEPTH)
    depth_pos = jnp.arange(N_DEPTH, dtype=jnp.int32)[:, None, None]
    distance = jnp.abs(depth_pos - centre)
    chance = jnp.maximum(15, 95 - 160 * distance // N_DEPTH)
    dice_rolls = jax.random.randint(key_rolls, (N_DEPTH, N_STRIP, TILES), 0, 100)
    return (dice_rolls < chance).astype(jnp.int32)


def touch_ends(values, rng, low, top_value):
    longest = values.shape.index(max(values.shape))
    spots = []
    for shift in (0, 1):
        where = [jax.random.randint(jax.random.fold_in(rng, axis), (), 0, length) for axis, length in enumerate(values.shape)]
        where[longest] = (where[longest] + shift) % values.shape[longest]
        spots.append(tuple(where))
    return values.at[spots[0]].set(low).at[spots[1]].set(top_value)


def block_scale(rng, extent, split, least, largest):
    def one(dim, parts):
        draws = jax.random.uniform(jax.random.fold_in(jax.random.fold_in(rng, 6), dim), (parts,), jnp.float32, least / len(split), largest / len(split))
        return jnp.repeat(jnp.exp(draws), extent[dim] // parts).reshape((-1,) + (1,) * (len(extent) - dim - 1))

    loudness = one(*split[0])
    for cut in split[1:]:
        loudness = loudness * one(*cut)
    return loudness


def centred(key, dims, spread, limit, split=(), held_as=jnp.bfloat16):
    values = jax.random.normal(key, dims, jnp.float32) * spread
    if len(split) > 0:
        values = block_scale(key, dims, split, -0.22, 0.18) * values
    return jnp.clip(values, min=-limit, max=limit).astype(held_as)


def setup_inputs(seed: int = 0) -> dict:
    seeds = jax.random.split(jax.random.key(seed), 6)
    density = centred(seeds[0], (NZ, NY, COLS), 1.0, 6.0, ((0, 8), (1, 4)), jnp.float32)
    materials = touch_ends(jax.random.randint(seeds[1], (NZ, NY, COLS), 0, MATS), jax.random.fold_in(seeds[1], 1), 0, MATS - 1).astype(jnp.int32)
    occupancy_flags = draw_occupancy_flags(jax.random.fold_in(seeds[5], 71), 0)
    tf_color = jnp.clip(jax.random.uniform(seeds[3], (MATS, 3, KNOTS), jnp.float32, 0.1, 1.0), 0.1, 1.0)
    tf_opacity = jnp.clip(jnp.exp(jax.random.uniform(seeds[4], (MATS, KNOTS), jnp.float32, math.log(0.0005), math.log(0.05))), 0.0005, 0.05)
    return dict(density=density, materials=materials, occupancy_flags=occupancy_flags, tf_color=tf_color, tf_opacity=tf_opacity)


light_x = 1.0 / 3.0
light_y = 2.0 / 3.0
light_z = 2.0 / 3.0
ambient = 0.3
diffuse = 0.7

def shade_slice(before, here, after, material_slice, occupied, knot_table):
    sample = here[1:-1, 1:-1]
    grad_z = 0.5 * (after[1:-1, 1:-1] - before[1:-1, 1:-1])
    grad_y = 0.5 * (here[2:, 1:-1] - here[:-2, 1:-1])
    grad_x = 0.5 * (here[1:-1, 2:] - here[1:-1, :-2])
    knot_count = knot_table.shape[1]
    material_count = knot_table.shape[0] // 4
    position = jnp.clip((sample.reshape(-1) + 3.0) * ((knot_count - 1) / 6.0), 0.0, knot_count - 1.0)
    knot_grid = jnp.arange(knot_count, dtype=jnp.float32)[:, None]
    tent_weights = jnp.maximum(0.0, 1.0 - jnp.abs(position[None, :] - knot_grid))
    looked = jnp.dot(knot_table, tent_weights, precision=lax.Precision.HIGHEST, preferred_element_type=jnp.float32)
    onehot = (material_slice.reshape(-1)[None, :] == jnp.arange(material_count, dtype=jnp.int32)[:, None]).astype(jnp.float32)
    colour = lax.optimization_barrier(jnp.sum(looked[:3 * material_count].reshape(material_count, 3, -1) * onehot[:, None, :], axis=0))
    density_rate = lax.optimization_barrier(jnp.sum(looked[3 * material_count:] * onehot, axis=0)) * occupied.reshape(-1)
    facing = (grad_x * light_x + grad_y * light_y + grad_z * light_z).reshape(-1)
    steepness = (grad_x * grad_x + grad_y * grad_y + grad_z * grad_z).reshape(-1)
    lighting = ambient + diffuse * jnp.abs(facing) / jnp.sqrt(1.0 + steepness)
    opacity_step = 1.0 - jnp.exp(-density_rate)
    return (colour * (lighting * opacity_step)[None, :], opacity_step)

def reference(density, materials, occupancy_flags, tf_color, tf_opacity):
    knot_table = jnp.concatenate([tf_color.reshape(MATS * 3, KNOTS), tf_opacity], axis=0)
    padded = jnp.pad(density, 1)

    def advance(state_carry, slab_index):
        radiance, transmit = state_carry
        before = lax.dynamic_index_in_dim(padded, slab_index, 0, keepdims=False)
        here = lax.dynamic_index_in_dim(padded, slab_index + 1, 0, keepdims=False)
        after = lax.dynamic_index_in_dim(padded, slab_index + 2, 0, keepdims=False)
        material_slice = lax.dynamic_index_in_dim(materials, slab_index, 0, keepdims=False)
        tile_flags = lax.dynamic_index_in_dim(occupancy_flags, slab_index // DZ, 0, keepdims=False)
        occupied = jnp.repeat(jnp.repeat(tile_flags, RY, axis=0), COLS // TILES, axis=1).astype(jnp.float32)
        emitted, opacity_step = shade_slice(before, here, after, material_slice, occupied, knot_table)
        return ((radiance + transmit[None, :] * emitted, transmit * (1.0 - opacity_step)), None)
    start = (jnp.zeros((3, NY * COLS), jnp.float32), jnp.ones((NY * COLS,), jnp.float32))
    (radiance, transmit), _ = lax.scan(advance, start, jnp.arange(NZ, dtype=jnp.int32))
    return jnp.concatenate([radiance.reshape(3, NY, COLS), (1.0 - transmit).reshape(1, NY, COLS)], axis=0)
```

```python
import functools

import jax
import jax.numpy as jnp
from jax import lax
from jax.experimental import pallas as pl
from jax.experimental.pallas import tpu as pltpu
from jax.sharding import PartitionSpec as P

ambient = 0.3
diffuse = 0.7
LANES = 128
ROWS = 8


def neighbours(count, first):
    pairs = []
    for low in range(first, count - 1, 2):
        pairs += [(low, low + 1), (low + 1, low)]
    return pairs


def halo(first, last, axis, exchange):
    count = lax.axis_size(axis)
    odd = lax.axis_index(axis) % 2 == 1
    inner = lax.ppermute(jnp.where(odd, first, last), axis, neighbours(count, 0))
    outer = lax.ppermute(jnp.where(odd, last, first), axis, neighbours(count, 1))
    return jnp.where(odd, inner, outer), jnp.where(odd, outer, inner)


def shade_kernel(tile_of, flags, density, materials, before, after, above, below, tables, out):
    slices, rows, columns = density.shape
    tiles = columns // LANES
    knots = tables.shape[1] // 8
    lane = lax.broadcasted_iota(jnp.int32, (ROWS, LANES), 1)
    row = lax.broadcasted_iota(jnp.int32, (ROWS, LANES), 0)
    table = [jnp.broadcast_to(tables[i : i + 1, :], (ROWS, LANES)) for i in range(4)]
    bands = rows // ROWS

    def body(i, _):
        c = tile_of[i]
        here = pl.ds(pl.multiple_of(c * LANES, LANES), LANES)
        left = pl.ds(pl.multiple_of(jnp.maximum(c - 1, 0) * LANES, LANES), LANES)
        right = pl.ds(pl.multiple_of(jnp.minimum(c + 1, tiles - 1) * LANES, LANES), LANES)
        has_left = jnp.where(c > 0, 1.0, 0.0)
        has_right = jnp.where(c < tiles - 1, 1.0, 0.0)
        occupied = flags[c].astype(jnp.float32)
        d = [[density[z, b * ROWS : (b + 1) * ROWS, here] for b in range(bands)] for z in range(slices)]
        radiance = [[None] * 3 for _ in range(bands)]
        transmit = [None] * bands
        for z in range(slices):
            up = [pltpu.roll(v, ROWS - 1, 0) for v in d[z]]
            down = [pltpu.roll(v, 1, 0) for v in d[z]]
            for b in range(bands):
                v = d[z][b]
                band = slice(b * ROWS, (b + 1) * ROWS)
                nearer = before[0, band, here] if z == 0 else d[z - 1][b]
                farther = after[0, band, here] if z == slices - 1 else d[z + 1][b]
                dz = farther - nearer
                top = down[b - 1] if b else jnp.broadcast_to(above[z, :, here], (ROWS, LANES))
                bottom = (
                    up[b + 1] if b < bands - 1 else jnp.broadcast_to(below[z, :, here], (ROWS, LANES))
                )
                dy = jnp.where(row == ROWS - 1, bottom, up[b]) - jnp.where(row == 0, top, down[b])
                vl = density[z, band, left] * has_left
                vr = density[z, band, right] * has_right
                dx = jnp.where(
                    lane == LANES - 1, pltpu.roll(vr, LANES - 1, 1), pltpu.roll(v, LANES - 1, 1)
                ) - jnp.where(lane == 0, pltpu.roll(vl, 1, 1), pltpu.roll(v, 1, 1))
                facing = jnp.abs(dx + 2.0 * (dy + dz))
                lighting = ambient + (diffuse / 3.0) * facing * lax.rsqrt(
                    4.0 + (dx * dx + dy * dy + dz * dz)
                )
                position = jnp.clip((v + 3.0) * ((knots - 1) / 6.0), 0.0, knots - 1.0)
                whole = position.astype(jnp.int32)
                part = position - whole.astype(jnp.float32)
                index = materials[z, band, here] * knots + whole
                slope_index = index + LANES // 2

                def look(t):
                    base = jnp.take_along_axis(t, index, axis=1, mode="promise_in_bounds")
                    slope = jnp.take_along_axis(t, slope_index, axis=1, mode="promise_in_bounds")
                    return base + part * slope

                rate = look(table[3]) * occupied
                clear = jnp.exp(-rate)
                weight = lighting * (1.0 - clear)
                if z:
                    weight = weight * transmit[b]
                for ch in range(3):
                    term = look(table[ch]) * weight
                    radiance[b][ch] = radiance[b][ch] + term if z else term
                transmit[b] = transmit[b] * clear if z else clear
        for b in range(bands):
            band = slice(b * ROWS, (b + 1) * ROWS)
            for ch in range(3):
                out[i, ch, band, :] = radiance[b][ch]
            out[i, 3, band, :] = transmit[b]
        return 0

    lax.fori_loop(0, out.shape[0], body, 0)


def shade(tile_of, flags, density, materials, before, after, above, below, tables):
    rows = density.shape[1]
    count = tile_of.shape[0]
    smem = pl.BlockSpec(memory_space=pltpu.SMEM)
    vmem = pl.BlockSpec(memory_space=pltpu.VMEM)
    return pl.pallas_call(
        shade_kernel,
        out_shape=jax.ShapeDtypeStruct((count, 4, rows, LANES), jnp.float32),
        in_specs=[smem, smem] + [vmem] * 7,
        out_specs=vmem,
        compiler_params=pltpu.CompilerParams(vmem_limit_bytes=16 * 1024 * 1024),
    )(tile_of, flags, density, materials, before, after, above, below, tables)


def composite_over(nearer, farther):
    return jnp.concatenate(
        [nearer[:, :3] + nearer[:, 3:] * farther[:, :3], nearer[:, 3:] * farther[:, 3:]], axis=1
    )


def lookup_tables(tf_color, tf_opacity):
    values = jnp.concatenate([tf_color.transpose(1, 0, 2), tf_opacity[None]], axis=0)
    steps = jnp.pad(values[:, :, 1:] - values[:, :, :-1], ((0, 0), (0, 0), (0, 1)))
    lanes = jnp.concatenate([values, steps], axis=1)
    return lanes.reshape(4, -1)


def on_device(density, materials, occupancy_flags, tf_color, tf_opacity):
    slices, rows, columns = density.shape
    before, after = halo(density[:1], density[-1:], "depth", None)
    above, below = halo(density[:, :1], density[:, -1:], "strip", None)
    tables = lookup_tables(tf_color, tf_opacity)
    tiles = columns // LANES
    groups = lax.axis_size("depth")
    width = columns // groups
    flags = occupancy_flags[0, 0]
    partial_value = shade(
        jnp.arange(tiles, dtype=jnp.int32), flags, density, materials, before, after, above, below, tables
    )
    if width % LANES == 0:
        pieces = lax.all_to_all(partial_value, "depth", split_axis=0, concat_axis=0, tiled=True)
        pieces = pieces.reshape(groups, width // LANES, 4, rows, LANES)
        pieces = pieces.transpose(0, 2, 3, 1, 4).reshape(groups, 4, rows, width)
    else:
        natural = partial_value.transpose(1, 2, 0, 3).reshape(4, rows, groups, width)
        pieces = lax.all_to_all(
            natural.transpose(2, 0, 1, 3), "depth", split_axis=0, concat_axis=0, tiled=True
        )
    while pieces.shape[0] > 1:
        pieces = composite_over(pieces[0::2], pieces[1::2])
    finished = pieces[0]
    return jnp.concatenate([finished[:3], 1.0 - finished[3:]], axis=0)


def solution(mesh):
    placed = (
        P("depth", "strip", None),
        P("depth", "strip", None),
        P("depth", "strip", None),
        P(),
        P(),
    )
    return jax.shard_map(
        on_device, mesh=mesh, in_specs=placed, out_specs=P(None, "strip", "depth"), check_vma=False
    )
```

```python
import functools

import jax
import jax.numpy as jnp
from jax import lax
from jax.experimental import pallas as pl
from jax.experimental.pallas import tpu as pltpu
from jax.sharding import PartitionSpec as P

ambient = 0.3
diffuse = 0.7
LANES = 128
ROWS = 8
VMEM = pl.BlockSpec(memory_space=pltpu.VMEM)
SMEM = pl.BlockSpec(memory_space=pltpu.SMEM)


def neighbours(count, first):
    pairs = []
    for low in range(first, count - 1, 2):
        pairs += [(low, low + 1), (low + 1, low)]
    return pairs


def sent_layers(first, last, axis):
    odd = lax.axis_index(axis) % 2 == 1
    return jnp.where(odd, first, last), jnp.where(odd, last, first)


def tile(c):
    return pl.ds(pl.multiple_of(c * LANES, LANES), LANES)


def call(kernel, out_shape, in_specs, cost):
    return pl.pallas_call(
        kernel,
        out_shape=out_shape,
        in_specs=in_specs,
        out_specs=jax.tree.map(lambda _: VMEM, out_shape),
        cost_estimate=pl.CostEstimate(flops=cost, bytes_accessed=cost, transcendentals=0),
        compiler_params=pltpu.CompilerParams(vmem_limit_bytes=16 * 1024 * 1024),
    )


def array(*shape):
    return jax.ShapeDtypeStruct(shape, jnp.float32)


def lookup_kernel(flags, density, materials, tables, out):
    slices, rows, columns = density.shape
    knots = tables.shape[1] // 8
    table = [jnp.broadcast_to(tables[i : i + 1, :], (ROWS, LANES)) for i in range(4)]

    def body(c, _):
        here = tile(c)
        occupied = flags[c].astype(jnp.float32)
        for b in range(rows // ROWS):
            band = slice(b * ROWS, (b + 1) * ROWS)
            transmit = None
            for z in range(slices):
                position = jnp.clip(
                    (density[z, band, here] + 3.0) * ((knots - 1) / 6.0), 0.0, knots - 1.0
                )
                whole = position.astype(jnp.int32)
                part = position - whole.astype(jnp.float32)
                index = materials[z, band, here] * knots + whole
                slope_index = index + LANES // 2

                def look(t):
                    base = jnp.take_along_axis(t, index, axis=1, mode="promise_in_bounds")
                    slope = jnp.take_along_axis(t, slope_index, axis=1, mode="promise_in_bounds")
                    return base + part * slope

                clear = jnp.exp(-(look(table[3]) * occupied))
                weight = 1.0 - clear
                if z:
                    weight = weight * transmit
                for ch in range(3):
                    out[c, z * 3 + ch, band, :] = look(table[ch]) * weight
                transmit = transmit * clear if z else clear
            out[c, slices * 3, band, :] = transmit
        return 0

    lax.fori_loop(0, columns // LANES, body, 0, unroll=4)


def shade_kernel(order, density, weights, near_z, far_z, near_y, far_y, out):
    slices, rows, columns = density.shape
    tiles = columns // LANES
    bands = rows // ROWS
    lane = lax.broadcasted_iota(jnp.int32, (ROWS, LANES), 1)
    row = lax.broadcasted_iota(jnp.int32, (ROWS, LANES), 0)
    odd_z = lax.axis_index("depth") % 2 == 1
    odd_y = lax.axis_index("strip") % 2 == 1

    def body(i, _):
        c = order(i)
        here, left, right = tile(c), tile(jnp.maximum(c - 1, 0)), tile(jnp.minimum(c + 1, tiles - 1))
        has_left = jnp.where(c > 0, 1.0, 0.0)
        has_right = jnp.where(c < tiles - 1, 1.0, 0.0)
        d = [[density[z, b * ROWS : (b + 1) * ROWS, here] for b in range(bands)] for z in range(slices)]
        for b in range(bands):
            band = slice(b * ROWS, (b + 1) * ROWS)
            radiance = [None] * 3
            for z in range(slices):
                v = d[z][b]
                if z == 0:
                    nearer = jnp.where(odd_z, near_z[0, band, here], far_z[0, band, here])
                else:
                    nearer = d[z - 1][b]
                if z == slices - 1:
                    farther = jnp.where(odd_z, far_z[0, band, here], near_z[0, band, here])
                else:
                    farther = d[z + 1][b]
                dz = farther - nearer
                if b == 0:
                    top = jnp.where(odd_y, near_y[z, :, here], far_y[z, :, here])
                    top = jnp.broadcast_to(top, (ROWS, LANES))
                else:
                    top = d[z][b - 1]
                if b == bands - 1:
                    bottom = jnp.where(odd_y, far_y[z, :, here], near_y[z, :, here])
                    bottom = jnp.broadcast_to(bottom, (ROWS, LANES))
                else:
                    bottom = d[z][b + 1]
                dy = pltpu.roll(jnp.where(row == 0, bottom, v), ROWS - 1, 0) - pltpu.roll(
                    jnp.where(row == ROWS - 1, top, v), 1, 0
                )
                vl = density[z, band, left] * has_left
                vr = density[z, band, right] * has_right
                dx = pltpu.roll(jnp.where(lane == 0, vr, v), LANES - 1, 1) - pltpu.roll(
                    jnp.where(lane == LANES - 1, vl, v), 1, 1
                )
                facing = jnp.abs(dx + 2.0 * (dy + dz))
                lighting = ambient + (diffuse / 3.0) * facing * lax.rsqrt(
                    4.0 + (dx * dx + dy * dy + dz * dz)
                )
                for ch in range(3):
                    term = weights[c, z * 3 + ch, band, :] * lighting
                    radiance[ch] = radiance[ch] + term if z else term
            for ch in range(3):
                out[i, ch, band, :] = radiance[ch]
            out[i, 3, band, :] = weights[c, slices * 3, band, :]
        return 0

    lax.fori_loop(0, out.shape[0], body, 0, unroll=2)


def over(swap, nearer, farther):
    first = [jnp.where(swap, f, n) for n, f in zip(nearer, farther)]
    second = [jnp.where(swap, n, f) for n, f in zip(nearer, farther)]
    return [first[ch] + first[3] * second[ch] for ch in range(3)] + [first[3] * second[3]]


def merge_kernel(kept, received, *outs):
    index = lax.axis_index("depth")
    odd = index % 2 == 1
    chip = index // 2
    per = outs[0].shape[0]
    for k, out in enumerate(outs):
        for h in range(per):
            at = (chip ^ k) * per + h
            mine = [kept[at, ch] for ch in range(4)]
            other = [received[at, ch] for ch in range(4)]
            for ch, value in enumerate(over(odd, mine, other)):
                out[h, ch] = value


def finish_kernel(*refs):
    pieces, out = refs[:-1], refs[-1]
    chip = lax.axis_index("depth") // 2
    for h in range(pieces[0].shape[0]):
        values = [[piece[h, ch] for ch in range(4)] for piece in pieces]
        bit = 0
        while len(values) > 1:
            swap = (chip >> bit) % 2 == 1
            values = [over(swap, values[k], values[k + 1]) for k in range(0, len(values), 2)]
            bit += 1
        here = slice(h * LANES, (h + 1) * LANES)
        for ch in range(3):
            out[ch, :, here] = values[0][ch]
        out[3, :, here] = 1.0 - values[0][3]


def composite_over(nearer, farther):
    return jnp.concatenate(
        [nearer[:, :3] + nearer[:, 3:] * farther[:, :3], nearer[:, 3:] * farther[:, 3:]], axis=1
    )


def lookup_tables(tf_color, tf_opacity):
    values = jnp.concatenate([tf_color.transpose(1, 0, 2), tf_opacity[None]], axis=0)
    steps = jnp.pad(values[:, :, 1:] - values[:, :, :-1], ((0, 0), (0, 0), (0, 1)))
    lanes = jnp.concatenate([values, steps], axis=1)
    return lanes.reshape(4, -1)


def on_device(density, materials, occupancy_flags, tf_color, tf_opacity):
    slices, rows, columns = density.shape
    tiles = columns // LANES
    groups, strips = lax.axis_size("depth"), lax.axis_size("strip")
    width = columns // groups
    chips = groups // 2

    inner, outer = sent_layers(density[:1], density[-1:], "depth")
    far_z = lax.ppermute(outer, "depth", neighbours(groups, 1))
    inner_y, outer_y = sent_layers(density[:, :1], density[:, -1:], "strip")
    near_y = lax.ppermute(inner_y, "strip", neighbours(strips, 0))
    far_y = lax.ppermute(outer_y, "strip", neighbours(strips, 1))
    near_z = lax.ppermute(inner, "depth", neighbours(groups, 0))

    tables = lookup_tables(tf_color, tf_opacity)
    weights = call(
        lookup_kernel, array(tiles, slices * 3 + 1, rows, LANES), [SMEM] + [VMEM] * 3, 8_000_000
    )(occupancy_flags[0, 0], density, materials, tables)
    lit = (density, weights, near_z, far_z, near_y, far_y)

    paired = groups % 2 == 0 and chips & (chips - 1) == 0 and width % LANES == 0
    if paired:
        per = width // LANES
        half = array(tiles // 2, 4, rows, LANES)

        def block_order(other):
            def order(i):
                parity = (lax.axis_index("depth") + other) % 2
                return (i // per * 2 + parity) * per + i % per

            return order

        sent, kept = (
            call(functools.partial(shade_kernel, block_order(other)), half, [VMEM] * 6, 2_000_000)(*lit)
            for other in (1, 0)
        )
        received = lax.ppermute(sent, "depth", [(i, i ^ 1) for i in range(groups)])
        blocks = call(
            merge_kernel, [array(per, 4, rows, LANES)] * chips, [VMEM] * 2, 1_000_000
        )(kept, received)
        pieces = [blocks[0]] + [
            lax.ppermute(blocks[k], "depth", [(i, i ^ (2 * k)) for i in range(groups)])
            for k in range(1, chips)
        ]
        return call(finish_kernel, array(4, rows, width), [VMEM] * chips, 1_000_000)(*pieces)

    partial_value = call(
        functools.partial(shade_kernel, lambda i: i), array(tiles, 4, rows, LANES), [VMEM] * 6, 4_000_000
    )(*lit)
    natural = partial_value.transpose(1, 2, 0, 3).reshape(4, rows, groups, width)
    pieces = lax.all_to_all(
        natural.transpose(2, 0, 1, 3), "depth", split_axis=0, concat_axis=0, tiled=True
    )
    while pieces.shape[0] > 1:
        pieces = composite_over(pieces[0::2], pieces[1::2])
    finished = pieces[0]
    return jnp.concatenate([finished[:3], 1.0 - finished[3:]], axis=0)


def solution(mesh):
    placed = (
        P("depth", "strip", None),
        P("depth", "strip", None),
        P("depth", "strip", None),
        P(),
        P(),
    )
    return jax.shard_map(
        on_device, mesh=mesh, in_specs=placed, out_specs=P(None, "strip", "depth"), check_vma=False
    )
```

```python
import functools

import jax
import jax.numpy as jnp
from jax import lax
from jax.experimental import pallas as pl
from jax.experimental.pallas import tpu as pltpu
from jax.sharding import PartitionSpec as P

ambient = 0.3
diffuse = 0.7
LANES = 128
ROWS = 8
VMEM = pl.BlockSpec(memory_space=pltpu.VMEM)


def inner_pairs(count):
    return [(i, i ^ 1) for i in range(count)]


def outer_pairs(groups, strips, axis):
    pairs = []
    for g in range(groups):
        for s in range(strips):
            if axis == "depth":
                to = (g, s ^ 1) if g in (0, groups - 1) else (g + 1 if g % 2 else g - 1, s)
            else:
                to = (g ^ 1, s) if s in (0, strips - 1) else (g, s + 1 if s % 2 else s - 1)
            pairs.append((g * strips + s, to[0] * strips + to[1]))
    return pairs


def tile(c):
    return pl.ds(pl.multiple_of(c * LANES, LANES), LANES)


def call(kernel, out_shape, in_specs, cost):
    return pl.pallas_call(
        kernel,
        out_shape=out_shape,
        in_specs=in_specs,
        out_specs=jax.tree.map(lambda _: VMEM, out_shape),
        cost_estimate=pl.CostEstimate(flops=cost, bytes_accessed=cost, transcendentals=0),
        compiler_params=pltpu.CompilerParams(vmem_limit_bytes=16 * 1024 * 1024),
    )


def array(*shape):
    return jax.ShapeDtypeStruct(shape, jnp.float32)


def load_kernel(*refs):
    given, held = refs[:5], refs[5:10]
    inner_z, outer_z, inner_y, outer_y, sems = refs[10:]
    copies = [pltpu.make_async_copy(x, y, sems.at[i]) for i, (x, y) in enumerate(zip(given, held))]
    for copy in copies:
        copy.start()
    density = held[0]
    slices, rows, columns = density.shape
    odd_z = lax.axis_index("depth") % 2
    odd_y = lax.axis_index("strip") % 2 == 1
    copies[0].wait()
    inner_z[0] = density[(slices - 1) * (1 - odd_z)]
    outer_z[0] = density[(slices - 1) * odd_z]
    for z in range(slices):
        first, last = density[z, :1, :], density[z, rows - 1 :, :]
        inner_y[z : z + 1, :] = jnp.where(odd_y, first, last)
        outer_y[z : z + 1, :] = jnp.where(odd_y, last, first)
    for copy in copies[1:]:
        copy.wait()


def by_lane(table):
    here = [table[m : m + 1, :] for m in range(table.shape[0])]
    last = table.shape[1] - 1
    further = [jnp.concatenate([t[:, 1:], t[:, last:]], axis=1) for t in here]
    return jnp.concatenate(here + here, axis=1), jnp.concatenate(further + further, axis=1)


def lookup_kernel(density, materials, flags, tf_color, tf_opacity, out):
    slices, rows, columns = density.shape
    knots = tf_opacity.shape[1]
    lane = lax.broadcasted_iota(jnp.int32, (1, LANES), 1)
    table = []
    for ch in range(3):
        value, further = by_lane(tf_color[ch])
        low = (further * 65535.0 + 0.5).astype(jnp.int32)
        high = jnp.floor((value * (32767.0 * 65536.0) - low.astype(jnp.float32)) * (1.0 / 65536.0) + 0.5)
        table.append(jnp.broadcast_to(high.astype(jnp.int32) * 65536 + low, (ROWS, LANES)))
    value, further = by_lane(tf_opacity[...])
    rates = jnp.broadcast_to(jnp.where(lane < LANES // 2, value, further - value), (ROWS, LANES))

    occupied = [flags[:, :].astype(jnp.float32)] * (LANES // flags.shape[1])
    occupied = jnp.broadcast_to(jnp.concatenate(occupied, axis=1), (ROWS, LANES))

    def look(t, index):
        return jnp.take_along_axis(t, index, axis=1, mode="promise_in_bounds")

    def body(c, _):
        here = tile(c)
        present = look(occupied, jnp.full((ROWS, LANES), c, jnp.int32))
        for b in range(rows // ROWS):
            band = slice(b * ROWS, (b + 1) * ROWS)
            transmit = None
            for z in range(slices):
                position = jnp.clip(
                    (density[z, band, here] + 3.0) * ((knots - 1) / 6.0), 0.0, knots - 1.0
                )
                whole = position.astype(jnp.int32)
                part = position - whole.astype(jnp.float32)
                index = materials[z, band, here] * knots + whole
                rate = look(rates, index) + part * look(rates, index + LANES // 2)
                clear = jnp.exp(-(rate * present))
                weight = 1.0 - clear
                if z:
                    weight = weight * transmit
                of_low = (part * weight) * (1.0 / 65535.0)
                of_high = (weight - part * weight) * (1.0 / (32767.0 * 65536.0))
                for ch in range(3):
                    both = look(table[ch], index)
                    low = (both & 65535).astype(jnp.float32)
                    out[c, z * 3 + ch, band, :] = both.astype(jnp.float32) * of_high + low * of_low
                transmit = transmit * clear if z else clear
            out[c, slices * 3, band, :] = transmit
        return 0

    lax.fori_loop(0, columns // LANES, body, 0, unroll=4)


def shade_kernel(order, density, weights, near_z, far_z, near_y, far_y, out):
    slices, rows, columns = density.shape
    tiles = columns // LANES
    bands = rows // ROWS
    lane = lax.broadcasted_iota(jnp.int32, (ROWS, LANES), 1)
    row = lax.broadcasted_iota(jnp.int32, (ROWS, LANES), 0)
    at_z, at_y = lax.axis_index("depth"), lax.axis_index("strip")
    odd_z, odd_y = at_z % 2 == 1, at_y % 2 == 1
    has_nearer = jnp.where(at_z > 0, 1.0, 0.0)
    has_farther = jnp.where(at_z < lax.axis_size("depth") - 1, 1.0, 0.0)
    has_top = jnp.where(at_y > 0, 1.0, 0.0)
    has_bottom = jnp.where(at_y < lax.axis_size("strip") - 1, 1.0, 0.0)

    def body(i, _):
        c = order(i)
        here, left, right = tile(c), tile(jnp.maximum(c - 1, 0)), tile(jnp.minimum(c + 1, tiles - 1))
        has_left = jnp.where(c > 0, 1.0, 0.0)
        has_right = jnp.where(c < tiles - 1, 1.0, 0.0)
        d = [[density[z, b * ROWS : (b + 1) * ROWS, here] for b in range(bands)] for z in range(slices)]
        for b in range(bands):
            band = slice(b * ROWS, (b + 1) * ROWS)
            radiance = [None] * 3
            for z in range(slices):
                v = d[z][b]
                if z == 0:
                    nearer = jnp.where(odd_z, near_z[0, band, here], far_z[0, band, here]) * has_nearer
                else:
                    nearer = d[z - 1][b]
                if z == slices - 1:
                    farther = jnp.where(odd_z, far_z[0, band, here], near_z[0, band, here]) * has_farther
                else:
                    farther = d[z + 1][b]
                dz = farther - nearer
                if b == 0:
                    top = jnp.where(odd_y, near_y[z : z + 1, here], far_y[z : z + 1, here])
                    top = jnp.broadcast_to(top * has_top, (ROWS, LANES))
                else:
                    top = d[z][b - 1]
                if b == bands - 1:
                    bottom = jnp.where(odd_y, far_y[z : z + 1, here], near_y[z : z + 1, here])
                    bottom = jnp.broadcast_to(bottom * has_bottom, (ROWS, LANES))
                else:
                    bottom = d[z][b + 1]
                dy = pltpu.roll(jnp.where(row == 0, bottom, v), ROWS - 1, 0) - pltpu.roll(
                    jnp.where(row == ROWS - 1, top, v), 1, 0
                )
                vl = density[z, band, left] * has_left
                vr = density[z, band, right] * has_right
                dx = pltpu.roll(jnp.where(lane == 0, vr, v), LANES - 1, 1) - pltpu.roll(
                    jnp.where(lane == LANES - 1, vl, v), 1, 1
                )
                facing = jnp.abs(dx + 2.0 * (dy + dz))
                lighting = ambient + (diffuse / 3.0) * facing * lax.rsqrt(
                    4.0 + (dx * dx + dy * dy + dz * dz)
                )
                for ch in range(3):
                    term = weights[c, z * 3 + ch, band, :] * lighting
                    radiance[ch] = radiance[ch] + term if z else term
            for ch in range(3):
                out[i, ch, band, :] = radiance[ch]
            out[i, 3, band, :] = weights[c, slices * 3, band, :]
        return 0

    lax.fori_loop(0, out.shape[0], body, 0, unroll=2)


def over(swap, nearer, farther):
    first = [jnp.where(swap, f, n) for n, f in zip(nearer, farther)]
    second = [jnp.where(swap, n, f) for n, f in zip(nearer, farther)]
    return [first[ch] + first[3] * second[ch] for ch in range(3)] + [first[3] * second[3]]


def merge_kernel(kept, received, *outs):
    index = lax.axis_index("depth")
    odd = index % 2 == 1
    chip = index // 2
    per = outs[0].shape[0]
    for k, out in enumerate(outs):
        for h in range(per):
            at = (chip ^ k) * per + h
            mine = [kept[at, ch] for ch in range(4)]
            other = [received[at, ch] for ch in range(4)]
            for ch, value in enumerate(over(odd, mine, other)):
                out[h, ch] = value


def finish_kernel(*refs):
    pieces, out = refs[:-1], refs[-1]
    chip = lax.axis_index("depth") // 2
    for h in range(pieces[0].shape[0]):
        values = [[piece[h, ch] for ch in range(4)] for piece in pieces]
        bit = 0
        while len(values) > 1:
            swap = (chip >> bit) % 2 == 1
            values = [over(swap, values[k], values[k + 1]) for k in range(0, len(values), 2)]
            bit += 1
        here = slice(h * LANES, (h + 1) * LANES)
        for ch in range(3):
            out[ch, :, here] = values[0][ch]
        out[3, :, here] = 1.0 - values[0][3]


def composite_over(nearer, farther):
    return jnp.concatenate(
        [nearer[:, :3] + nearer[:, 3:] * farther[:, :3], nearer[:, 3:] * farther[:, 3:]], axis=1
    )


def on_device(density, materials, occupancy_flags, tf_color, tf_opacity):
    slices, rows, columns = density.shape
    tiles = columns // LANES
    groups, strips = lax.axis_size("depth"), lax.axis_size("strip")
    width = columns // groups
    chips = groups // 2

    given = (density, materials, occupancy_flags[0], tf_color.transpose(1, 0, 2), tf_opacity)
    layer, edge = array(1, rows, columns), array(slices, columns)
    density, materials, flags, tf_color, tf_opacity, inner_z, outer_z, inner_y, outer_y = pl.pallas_call(
        load_kernel,
        out_shape=[jax.ShapeDtypeStruct(x.shape, x.dtype) for x in given] + [layer, layer, edge, edge],
        in_specs=[pl.BlockSpec(memory_space=pltpu.HBM)] * 5,
        out_specs=[VMEM] * 9,
        scratch_shapes=[pltpu.SemaphoreType.DMA((5,))],
        compiler_params=pltpu.CompilerParams(vmem_limit_bytes=16 * 1024 * 1024),
    )(*[pltpu.with_memory_space_constraint(x, pltpu.HBM) for x in given])
    both = ("depth", "strip")
    far_z = lax.ppermute(outer_z, both, outer_pairs(groups, strips, "depth"))
    near_z = lax.ppermute(inner_z, "depth", inner_pairs(groups))
    near_y = lax.ppermute(inner_y, "strip", inner_pairs(strips))
    far_y = lax.ppermute(outer_y, both, outer_pairs(groups, strips, "strip"))

    weights = call(
        lookup_kernel, array(tiles, slices * 3 + 1, rows, LANES), [VMEM] * 5, 8_000_000
    )(density, materials, flags, tf_color, tf_opacity)
    lit = (density, weights, near_z, far_z, near_y, far_y)

    paired = groups % 2 == 0 and chips & (chips - 1) == 0 and width % LANES == 0
    if paired:
        per = width // LANES
        half = array(tiles // 2, 4, rows, LANES)

        def block_order(other):
            def order(i):
                parity = (lax.axis_index("depth") + other) % 2
                return (i // per * 2 + parity) * per + i % per

            return order

        sent, kept = (
            call(functools.partial(shade_kernel, block_order(other)), half, [VMEM] * 6, 2_000_000)(*lit)
            for other in (1, 0)
        )
        received = lax.ppermute(sent, "depth", inner_pairs(groups))
        blocks = call(
            merge_kernel, [array(per, 4, rows, LANES)] * chips, [VMEM] * 2, 1_000_000
        )(kept, received)
        pieces = [blocks[0]] + [
            lax.ppermute(blocks[k], "depth", [(i, i ^ (2 * k)) for i in range(groups)])
            for k in range(1, chips)
        ]
        return call(finish_kernel, array(4, rows, width), [VMEM] * chips, 1_000_000)(*pieces)

    partial_value = call(
        functools.partial(shade_kernel, lambda i: i), array(tiles, 4, rows, LANES), [VMEM] * 6, 4_000_000
    )(*lit)
    natural = partial_value.transpose(1, 2, 0, 3).reshape(4, rows, groups, width)
    pieces = lax.all_to_all(
        natural.transpose(2, 0, 1, 3), "depth", split_axis=0, concat_axis=0, tiled=True
    )
    while pieces.shape[0] > 1:
        pieces = composite_over(pieces[0::2], pieces[1::2])
    finished = pieces[0]
    return jnp.concatenate([finished[:3], 1.0 - finished[3:]], axis=0)


def solution(mesh):
    placed = (
        P("depth", "strip", None),
        P("depth", "strip", None),
        P("depth", "strip", None),
        P(),
        P(),
    )
    return jax.shard_map(
        on_device, mesh=mesh, in_specs=placed, out_specs=P(None, "strip", "depth"), check_vma=False
    )
```

```python
import functools

import jax
import jax.numpy as jnp
from jax import lax
from jax.experimental import pallas as pl
from jax.experimental.pallas import tpu as pltpu
from jax.sharding import PartitionSpec as P

ambient = 0.3
diffuse = 0.7
LANES = 128
ROWS = 8
VMEM = pl.BlockSpec(memory_space=pltpu.VMEM)


def inner_pairs(count):
    return [(i, i ^ 1) for i in range(count)]


def outer_pairs(groups, strips, axis):
    pairs = []
    for g in range(groups):
        for s in range(strips):
            if axis == "depth":
                to = (g, s ^ 1) if g in (0, groups - 1) else (g + 1 if g % 2 else g - 1, s)
            else:
                to = (g ^ 1, s) if s in (0, strips - 1) else (g, s + 1 if s % 2 else s - 1)
            pairs.append((g * strips + s, to[0] * strips + to[1]))
    return pairs


def tile(c):
    return pl.ds(pl.multiple_of(c * LANES, LANES), LANES)


def call(kernel, out_shape, in_specs, cost):
    return pl.pallas_call(
        kernel,
        out_shape=out_shape,
        in_specs=in_specs,
        out_specs=jax.tree.map(lambda _: VMEM, out_shape),
        cost_estimate=pl.CostEstimate(flops=cost, bytes_accessed=cost, transcendentals=0),
        compiler_params=pltpu.CompilerParams(vmem_limit_bytes=16 * 1024 * 1024),
    )


def array(*shape):
    return jax.ShapeDtypeStruct(shape, jnp.float32)


def load_kernel(*refs):
    given, held = refs[:5], refs[5:10]
    inner_z, outer_z, inner_y, outer_y, sems = refs[10:]
    copies = [pltpu.make_async_copy(x, y, sems.at[i]) for i, (x, y) in enumerate(zip(given, held))]
    for copy in copies:
        copy.start()
    density = held[0]
    slices, rows, columns = density.shape
    odd_z = lax.axis_index("depth") % 2
    odd_y = lax.axis_index("strip") % 2 == 1
    copies[0].wait()
    inner_z[0] = density[(slices - 1) * (1 - odd_z)]
    outer_z[0] = density[(slices - 1) * odd_z]
    for z in range(slices):
        first, last = density[z, :1, :], density[z, rows - 1 :, :]
        inner_y[z : z + 1, :] = jnp.where(odd_y, first, last)
        outer_y[z : z + 1, :] = jnp.where(odd_y, last, first)
    for copy in copies[1:]:
        copy.wait()


def by_lane(table):
    here = [table[m : m + 1, :] for m in range(table.shape[0])]
    last = table.shape[1] - 1
    further = [jnp.concatenate([t[:, 1:], t[:, last:]], axis=1) for t in here]
    return jnp.concatenate(here + here, axis=1), jnp.concatenate(further + further, axis=1)


def lookup_kernel(density, materials, flags, tf_color, tf_opacity, out):
    slices, rows, columns = density.shape
    knots = tf_opacity.shape[1]
    lane = lax.broadcasted_iota(jnp.int32, (1, LANES), 1)
    table = []
    for ch in range(3):
        value, further = by_lane(tf_color[ch])
        low = (further * 65535.0 + 0.5).astype(jnp.int32)
        high = jnp.floor((value * (32767.0 * 65536.0) - low.astype(jnp.float32)) * (1.0 / 65536.0) + 0.5)
        table.append(jnp.broadcast_to(high.astype(jnp.int32) * 65536 + low, (ROWS, LANES)))
    value, further = by_lane(tf_opacity[...])
    rates = jnp.broadcast_to(jnp.where(lane < LANES // 2, value, further - value), (ROWS, LANES))

    occupied = [flags[:, :].astype(jnp.float32)] * (LANES // flags.shape[1])
    occupied = jnp.broadcast_to(jnp.concatenate(occupied, axis=1), (ROWS, LANES))

    def look(t, index):
        return jnp.take_along_axis(t, index, axis=1, mode="promise_in_bounds")

    def body(c, _):
        here = tile(c)
        present = look(occupied, jnp.full((ROWS, LANES), c, jnp.int32))
        for b in range(rows // ROWS):
            band = slice(b * ROWS, (b + 1) * ROWS)
            transmit = None
            for z in range(slices):
                position = jnp.clip(
                    (density[z, band, here] + 3.0) * ((knots - 1) / 6.0), 0.0, knots - 1.0
                )
                whole = position.astype(jnp.int32)
                part = position - whole.astype(jnp.float32)
                index = materials[z, band, here] * knots + whole
                rate = look(rates, index) + part * look(rates, index + LANES // 2)
                clear = jnp.exp(-(rate * present))
                weight = 1.0 - clear
                if z:
                    weight = weight * transmit
                of_low = (part * weight) * (1.0 / 65535.0)
                of_high = (weight - part * weight) * (1.0 / (32767.0 * 65536.0))
                for ch in range(3):
                    both = look(table[ch], index)
                    low = (both & 65535).astype(jnp.float32)
                    out[c, z * 3 + ch, band, :] = both.astype(jnp.float32) * of_high + low * of_low
                transmit = transmit * clear if z else clear
            out[c, slices * 3, band, :] = transmit
        return 0

    lax.fori_loop(0, columns // LANES, body, 0, unroll=4)


def shade_kernel(order, density, weights, near_z, far_z, near_y, far_y, out):
    slices, rows, columns = density.shape
    tiles = columns // LANES
    bands = rows // ROWS
    lane = lax.broadcasted_iota(jnp.int32, (ROWS, LANES), 1)
    row = lax.broadcasted_iota(jnp.int32, (ROWS, LANES), 0)
    at_z, at_y = lax.axis_index("depth"), lax.axis_index("strip")
    odd_z, odd_y = at_z % 2 == 1, at_y % 2 == 1
    has_nearer = jnp.where(at_z > 0, 1.0, 0.0)
    has_farther = jnp.where(at_z < lax.axis_size("depth") - 1, 1.0, 0.0)
    has_top = jnp.where(at_y > 0, 1.0, 0.0)
    has_bottom = jnp.where(at_y < lax.axis_size("strip") - 1, 1.0, 0.0)

    def body(i, _):
        c = order(i)
        here, left, right = tile(c), tile(jnp.maximum(c - 1, 0)), tile(jnp.minimum(c + 1, tiles - 1))
        has_left = jnp.where(c > 0, 1.0, 0.0)
        has_right = jnp.where(c < tiles - 1, 1.0, 0.0)
        d = [[density[z, b * ROWS : (b + 1) * ROWS, here] for b in range(bands)] for z in range(slices)]
        for b in range(bands):
            band = slice(b * ROWS, (b + 1) * ROWS)
            radiance = [None] * 3
            for z in range(slices):
                v = d[z][b]
                if z == 0:
                    nearer = jnp.where(odd_z, near_z[0, band, here], far_z[0, band, here]) * has_nearer
                else:
                    nearer = d[z - 1][b]
                if z == slices - 1:
                    farther = jnp.where(odd_z, far_z[0, band, here], near_z[0, band, here]) * has_farther
                else:
                    farther = d[z + 1][b]
                dz = farther - nearer
                if b == 0:
                    top = jnp.where(odd_y, near_y[z : z + 1, here], far_y[z : z + 1, here])
                    top = jnp.broadcast_to(top * has_top, (ROWS, LANES))
                else:
                    top = d[z][b - 1]
                if b == bands - 1:
                    bottom = jnp.where(odd_y, far_y[z : z + 1, here], near_y[z : z + 1, here])
                    bottom = jnp.broadcast_to(bottom * has_bottom, (ROWS, LANES))
                else:
                    bottom = d[z][b + 1]
                dy = pltpu.roll(jnp.where(row == 0, bottom, v), ROWS - 1, 0) - pltpu.roll(
                    jnp.where(row == ROWS - 1, top, v), 1, 0
                )
                vl = density[z, band, left] * has_left
                vr = density[z, band, right] * has_right
                dx = pltpu.roll(jnp.where(lane == 0, vr, v), LANES - 1, 1) - pltpu.roll(
                    jnp.where(lane == LANES - 1, vl, v), 1, 1
                )
                facing = jnp.abs(dx + 2.0 * (dy + dz))
                lighting = ambient + (diffuse / 3.0) * facing * lax.rsqrt(
                    4.0 + (dx * dx + dy * dy + dz * dz)
                )
                for ch in range(3):
                    term = weights[c, z * 3 + ch, band, :] * lighting
                    radiance[ch] = radiance[ch] + term if z else term
            for ch in range(3):
                out[i, ch, band, :] = radiance[ch]
            out[i, 3, band, :] = weights[c, slices * 3, band, :]
        return 0

    lax.fori_loop(0, out.shape[0], body, 0, unroll=2)


def over(swap, nearer, farther):
    first = [jnp.where(swap, f, n) for n, f in zip(nearer, farther)]
    second = [jnp.where(swap, n, f) for n, f in zip(nearer, farther)]
    return [first[ch] + first[3] * second[ch] for ch in range(3)] + [first[3] * second[3]]


def merge_kernel(kept, received, *outs):
    index = lax.axis_index("depth")
    odd = index % 2 == 1
    chip = index // 2
    per = outs[0].shape[0]
    for k, out in enumerate(outs):
        for h in range(per):
            at = (chip ^ k) * per + h
            mine = [kept[at, ch] for ch in range(4)]
            other = [received[at, ch] for ch in range(4)]
            for ch, value in enumerate(over(odd, mine, other)):
                out[h, ch] = value


def finish_order(chips):
    return [0] + sorted(range(1, chips), key=lambda k: (-k.bit_count(), k))


def finish_kernel(*refs):
    given, out = dict(zip(finish_order(len(refs) - 1), refs)), refs[-1]
    pieces = [given[k] for k in range(len(given))]
    chip = lax.axis_index("depth") // 2
    for h in range(pieces[0].shape[0]):
        values = [[piece[h, ch] for ch in range(4)] for piece in pieces]
        bit = 0
        while len(values) > 1:
            swap = (chip >> bit) % 2 == 1
            values = [over(swap, values[k], values[k + 1]) for k in range(0, len(values), 2)]
            bit += 1
        here = slice(h * LANES, (h + 1) * LANES)
        for ch in range(3):
            out[ch, :, here] = values[0][ch]
        out[3, :, here] = 1.0 - values[0][3]


def composite_over(nearer, farther):
    return jnp.concatenate(
        [nearer[:, :3] + nearer[:, 3:] * farther[:, :3], nearer[:, 3:] * farther[:, 3:]], axis=1
    )


def on_device(density, materials, occupancy_flags, tf_color, tf_opacity):
    slices, rows, columns = density.shape
    tiles = columns // LANES
    groups, strips = lax.axis_size("depth"), lax.axis_size("strip")
    width = columns // groups
    chips = groups // 2

    given = (density, materials, occupancy_flags[0], tf_color.transpose(1, 0, 2), tf_opacity)
    layer, edge = array(1, rows, columns), array(slices, columns)
    density, materials, flags, tf_color, tf_opacity, inner_z, outer_z, inner_y, outer_y = pl.pallas_call(
        load_kernel,
        out_shape=[jax.ShapeDtypeStruct(x.shape, x.dtype) for x in given] + [layer, layer, edge, edge],
        in_specs=[pl.BlockSpec(memory_space=pltpu.HBM)] * 5,
        out_specs=[VMEM] * 9,
        scratch_shapes=[pltpu.SemaphoreType.DMA((5,))],
        compiler_params=pltpu.CompilerParams(vmem_limit_bytes=16 * 1024 * 1024),
    )(*[pltpu.with_memory_space_constraint(x, pltpu.HBM) for x in given])
    both = ("depth", "strip")
    far_z = lax.ppermute(outer_z, both, outer_pairs(groups, strips, "depth"))
    near_z = lax.ppermute(inner_z, "depth", inner_pairs(groups))
    near_y = lax.ppermute(inner_y, "strip", inner_pairs(strips))
    far_y = lax.ppermute(outer_y, both, outer_pairs(groups, strips, "strip"))

    weights = call(
        lookup_kernel, array(tiles, slices * 3 + 1, rows, LANES), [VMEM] * 5, 8_000_000
    )(density, materials, flags, tf_color, tf_opacity)
    lit = (density, weights, near_z, far_z, near_y, far_y)

    paired = groups % 2 == 0 and chips & (chips - 1) == 0 and width % LANES == 0
    if paired:
        per = width // LANES
        half = array(tiles // 2, 4, rows, LANES)

        def block_order(other):
            def order(i):
                parity = (lax.axis_index("depth") + other) % 2
                return (i // per * 2 + parity) * per + i % per

            return order

        sent, kept = (
            call(functools.partial(shade_kernel, block_order(other)), half, [VMEM] * 6, 2_000_000)(*lit)
            for other in (1, 0)
        )
        received = lax.ppermute(sent, "depth", inner_pairs(groups))
        blocks = call(
            merge_kernel, [array(per, 4, rows, LANES)] * chips, [VMEM] * 2, 1_000_000
        )(kept, received)
        pieces = [blocks[0]] + [
            lax.ppermute(blocks[k], "depth", [(i, i ^ (2 * k)) for i in range(groups)])
            for k in range(1, chips)
        ]
        return call(finish_kernel, array(4, rows, width), [VMEM] * chips, 1_000_000)(*[pieces[k] for k in finish_order(chips)])

    partial_value = call(
        functools.partial(shade_kernel, lambda i: i), array(tiles, 4, rows, LANES), [VMEM] * 6, 4_000_000
    )(*lit)
    natural = partial_value.transpose(1, 2, 0, 3).reshape(4, rows, groups, width)
    pieces = lax.all_to_all(
        natural.transpose(2, 0, 1, 3), "depth", split_axis=0, concat_axis=0, tiled=True
    )
    while pieces.shape[0] > 1:
        pieces = composite_over(pieces[0::2], pieces[1::2])
    finished = pieces[0]
    return jnp.concatenate([finished[:3], 1.0 - finished[3:]], axis=0)


def solution(mesh):
    placed = (
        P("depth", "strip", None),
        P("depth", "strip", None),
        P("depth", "strip", None),
        P(),
        P(),
    )
    return jax.shard_map(
        on_device, mesh=mesh, in_specs=placed, out_specs=P(None, "strip", "depth"), check_vma=False
    )
```

```python
import functools

import jax
import jax.numpy as jnp
from jax import lax
from jax.experimental import pallas as pl
from jax.experimental.pallas import tpu as pltpu
from jax.sharding import PartitionSpec as P

ambient = 0.3
diffuse = 0.7
LANES = 128
ROWS = 8
VMEM = pl.BlockSpec(memory_space=pltpu.VMEM)


def inner_pairs(count):
    return [(i, i ^ 1) for i in range(count)]


def outer_pairs(groups, strips, axis):
    pairs = []
    for g in range(groups):
        for s in range(strips):
            if axis == "depth":
                to = (g, s ^ 1) if g in (0, groups - 1) else (g + 1 if g % 2 else g - 1, s)
            else:
                to = (g ^ 1, s) if s in (0, strips - 1) else (g, s + 1 if s % 2 else s - 1)
            pairs.append((g * strips + s, to[0] * strips + to[1]))
    return pairs


def tile(c):
    return pl.ds(pl.multiple_of(c * LANES, LANES), LANES)


def call(kernel, out_shape, in_specs, cost):
    return pl.pallas_call(
        kernel,
        out_shape=out_shape,
        in_specs=in_specs,
        out_specs=jax.tree.map(lambda _: VMEM, out_shape),
        cost_estimate=pl.CostEstimate(flops=cost, bytes_accessed=cost, transcendentals=0),
        compiler_params=pltpu.CompilerParams(vmem_limit_bytes=16 * 1024 * 1024),
    )


def array(*shape):
    return jax.ShapeDtypeStruct(shape, jnp.float32)


def load_kernel(*refs):
    given, held = refs[:5], refs[5:10]
    inner_z, outer_z, inner_y, outer_y, sems = refs[10:]
    copies = [pltpu.make_async_copy(x, y, sems.at[i]) for i, (x, y) in enumerate(zip(given, held))]
    for copy in copies:
        copy.start()
    density = held[0]
    slices, rows, columns = density.shape
    odd_z = lax.axis_index("depth") % 2
    odd_y = lax.axis_index("strip") % 2 == 1
    copies[0].wait()
    inner_z[0] = density[(slices - 1) * (1 - odd_z)]
    outer_z[0] = density[(slices - 1) * odd_z]
    for z in range(slices):
        first, last = density[z, :1, :], density[z, rows - 1 :, :]
        inner_y[z : z + 1, :] = jnp.where(odd_y, first, last)
        outer_y[z : z + 1, :] = jnp.where(odd_y, last, first)
    for copy in copies[1:]:
        copy.wait()


def by_lane(table):
    here = [table[m : m + 1, :] for m in range(table.shape[0])]
    last = table.shape[1] - 1
    further = [jnp.concatenate([t[:, 1:], t[:, last:]], axis=1) for t in here]
    return jnp.concatenate(here + here, axis=1), jnp.concatenate(further + further, axis=1)


def lookup_kernel(density, materials, flags, tf_color, tf_opacity, out):
    slices, rows, columns = density.shape
    knots = tf_opacity.shape[1]
    lane = lax.broadcasted_iota(jnp.int32, (1, LANES), 1)
    table = []
    for ch in range(3):
        value, further = by_lane(tf_color[ch])
        low = (further * 65535.0 + 0.5).astype(jnp.int32)
        high = jnp.floor((value * (32767.0 * 65536.0) - low.astype(jnp.float32)) * (1.0 / 65536.0) + 0.5)
        table.append(jnp.broadcast_to(high.astype(jnp.int32) * 65536 + low, (ROWS, LANES)))
    value, further = by_lane(tf_opacity[...])
    rates = jnp.broadcast_to(jnp.where(lane < LANES // 2, value, further - value), (ROWS, LANES))

    occupied = [flags[:, :].astype(jnp.float32)] * (LANES // flags.shape[1])
    occupied = jnp.broadcast_to(jnp.concatenate(occupied, axis=1), (ROWS, LANES))

    def look(t, index):
        return jnp.take_along_axis(t, index, axis=1, mode="promise_in_bounds")

    def body(c, _):
        here = tile(c)
        present = look(occupied, jnp.full((ROWS, LANES), c, jnp.int32))
        for b in range(rows // ROWS):
            band = slice(b * ROWS, (b + 1) * ROWS)
            transmit = None
            for z in range(slices):
                position = jnp.clip(
                    (density[z, band, here] + 3.0) * ((knots - 1) / 6.0), 0.0, knots - 1.0
                )
                whole = position.astype(jnp.int32)
                part = position - whole.astype(jnp.float32)
                index = materials[z, band, here] * knots + whole
                rate = look(rates, index) + part * look(rates, index + LANES // 2)
                clear = jnp.exp(-(rate * present))
                weight = 1.0 - clear
                if z:
                    weight = weight * transmit
                of_low = (part * weight) * (1.0 / 65535.0)
                of_high = (weight - part * weight) * (1.0 / (32767.0 * 65536.0))
                for ch in range(3):
                    both = look(table[ch], index)
                    low = (both & 65535).astype(jnp.float32)
                    out[c, z * 3 + ch, band, :] = both.astype(jnp.float32) * of_high + low * of_low
                transmit = transmit * clear if z else clear
            out[c, slices * 3, band, :] = transmit
        return 0

    lax.fori_loop(0, columns // LANES, body, 0, unroll=16)


def shade_kernel(order, density, weights, far_z, near_y, far_y, near_z, out):
    slices, rows, columns = density.shape
    tiles = columns // LANES
    bands = rows // ROWS
    lane = lax.broadcasted_iota(jnp.int32, (ROWS, LANES), 1)
    row = lax.broadcasted_iota(jnp.int32, (ROWS, LANES), 0)
    at_z, at_y = lax.axis_index("depth"), lax.axis_index("strip")
    odd_z, odd_y = at_z % 2 == 1, at_y % 2 == 1
    has_nearer = jnp.where(at_z > 0, 1.0, 0.0)
    has_farther = jnp.where(at_z < lax.axis_size("depth") - 1, 1.0, 0.0)
    has_top = jnp.where(at_y > 0, 1.0, 0.0)
    has_bottom = jnp.where(at_y < lax.axis_size("strip") - 1, 1.0, 0.0)

    def body(i, _):
        c = order(i)
        here, left, right = tile(c), tile(jnp.maximum(c - 1, 0)), tile(jnp.minimum(c + 1, tiles - 1))
        has_left = jnp.where(c > 0, 1.0, 0.0)
        has_right = jnp.where(c < tiles - 1, 1.0, 0.0)
        d = [[density[z, b * ROWS : (b + 1) * ROWS, here] for b in range(bands)] for z in range(slices)]
        for b in range(bands):
            band = slice(b * ROWS, (b + 1) * ROWS)
            radiance = [None] * 3
            for z in range(slices):
                v = d[z][b]
                if z == 0:
                    nearer = jnp.where(odd_z, near_z[0, band, here], far_z[0, band, here]) * has_nearer
                else:
                    nearer = d[z - 1][b]
                if z == slices - 1:
                    farther = jnp.where(odd_z, far_z[0, band, here], near_z[0, band, here]) * has_farther
                else:
                    farther = d[z + 1][b]
                dz = farther - nearer
                if b == 0:
                    top = jnp.where(odd_y, near_y[z : z + 1, here], far_y[z : z + 1, here])
                    top = jnp.broadcast_to(top * has_top, (ROWS, LANES))
                else:
                    top = d[z][b - 1]
                if b == bands - 1:
                    bottom = jnp.where(odd_y, far_y[z : z + 1, here], near_y[z : z + 1, here])
                    bottom = jnp.broadcast_to(bottom * has_bottom, (ROWS, LANES))
                else:
                    bottom = d[z][b + 1]
                dy = pltpu.roll(jnp.where(row == 0, bottom, v), ROWS - 1, 0) - pltpu.roll(
                    jnp.where(row == ROWS - 1, top, v), 1, 0
                )
                vl = density[z, band, left] * has_left
                vr = density[z, band, right] * has_right
                dx = pltpu.roll(jnp.where(lane == 0, vr, v), LANES - 1, 1) - pltpu.roll(
                    jnp.where(lane == LANES - 1, vl, v), 1, 1
                )
                facing = jnp.abs(dx + 2.0 * (dy + dz))
                lighting = ambient + (diffuse / 3.0) * facing * lax.rsqrt(
                    4.0 + (dx * dx + dy * dy + dz * dz)
                )
                for ch in range(3):
                    term = weights[c, z * 3 + ch, band, :] * lighting
                    radiance[ch] = radiance[ch] + term if z else term
            for ch in range(3):
                out[i, ch, band, :] = radiance[ch]
            out[i, 3, band, :] = weights[c, slices * 3, band, :]
        return 0

    lax.fori_loop(0, out.shape[0], body, 0, unroll=8)


def over(swap, nearer, farther):
    first = [jnp.where(swap, f, n) for n, f in zip(nearer, farther)]
    second = [jnp.where(swap, n, f) for n, f in zip(nearer, farther)]
    return [first[ch] + first[3] * second[ch] for ch in range(3)] + [first[3] * second[3]]


def merge_kernel(kept, received, *outs):
    index = lax.axis_index("depth")
    odd = index % 2 == 1
    chip = index // 2
    per = outs[0].shape[0]
    for k, out in enumerate(outs):
        for h in range(per):
            at = (chip ^ k) * per + h
            mine = [kept[at, ch] for ch in range(4)]
            other = [received[at, ch] for ch in range(4)]
            for ch, value in enumerate(over(odd, mine, other)):
                out[h, ch] = value


def finish_order(chips):
    return [0] + sorted(range(1, chips), key=lambda k: (-k.bit_count(), k))


def finish_kernel(*refs):
    given, out = dict(zip(finish_order(len(refs) - 1), refs)), refs[-1]
    pieces = [given[k] for k in range(len(given))]
    chip = lax.axis_index("depth") // 2
    for h in range(pieces[0].shape[0]):
        values = [[piece[h, ch] for ch in range(4)] for piece in pieces]
        bit = 0
        while len(values) > 1:
            swap = (chip >> bit) % 2 == 1
            values = [over(swap, values[k], values[k + 1]) for k in range(0, len(values), 2)]
            bit += 1
        here = slice(h * LANES, (h + 1) * LANES)
        for ch in range(3):
            out[ch, :, here] = values[0][ch]
        out[3, :, here] = 1.0 - values[0][3]


def composite_over(nearer, farther):
    return jnp.concatenate(
        [nearer[:, :3] + nearer[:, 3:] * farther[:, :3], nearer[:, 3:] * farther[:, 3:]], axis=1
    )


def on_device(density, materials, occupancy_flags, tf_color, tf_opacity):
    slices, rows, columns = density.shape
    tiles = columns // LANES
    groups, strips = lax.axis_size("depth"), lax.axis_size("strip")
    width = columns // groups
    chips = groups // 2

    given = (density, materials, occupancy_flags[0], tf_color.transpose(1, 0, 2), tf_opacity)
    layer, edge = array(1, rows, columns), array(slices, columns)
    density, materials, flags, tf_color, tf_opacity, inner_z, outer_z, inner_y, outer_y = pl.pallas_call(
        load_kernel,
        out_shape=[jax.ShapeDtypeStruct(x.shape, x.dtype) for x in given] + [layer, layer, edge, edge],
        in_specs=[pl.BlockSpec(memory_space=pltpu.HBM)] * 5,
        out_specs=[VMEM] * 9,
        scratch_shapes=[pltpu.SemaphoreType.DMA((5,))],
        compiler_params=pltpu.CompilerParams(vmem_limit_bytes=16 * 1024 * 1024),
    )(*[pltpu.with_memory_space_constraint(x, pltpu.HBM) for x in given])
    both = ("depth", "strip")
    far_z = lax.ppermute(outer_z, both, outer_pairs(groups, strips, "depth"))
    near_z = lax.ppermute(inner_z, "depth", inner_pairs(groups))
    near_y = lax.ppermute(inner_y, "strip", inner_pairs(strips))
    far_y = lax.ppermute(outer_y, both, outer_pairs(groups, strips, "strip"))

    weights = call(
        lookup_kernel, array(tiles, slices * 3 + 1, rows, LANES), [VMEM] * 5, 8_000_000
    )(density, materials, flags, tf_color, tf_opacity)
    lit = (density, weights, far_z, near_y, far_y, near_z)

    paired = groups % 2 == 0 and chips & (chips - 1) == 0 and width % LANES == 0
    if paired:
        per = width // LANES
        half = array(tiles // 2, 4, rows, LANES)

        def block_order(other):
            def order(i):
                parity = (lax.axis_index("depth") + other) % 2
                return (i // per * 2 + parity) * per + i % per

            return order

        sent, kept = (
            call(functools.partial(shade_kernel, block_order(other)), half, [VMEM] * 6, 2_000_000)(*lit)
            for other in (1, 0)
        )
        received = lax.ppermute(sent, "depth", inner_pairs(groups))
        blocks = call(
            merge_kernel, [array(per, 4, rows, LANES)] * chips, [VMEM] * 2, 1_000_000
        )(kept, received)
        pieces = [blocks[0]] + [
            lax.ppermute(blocks[k], "depth", [(i, i ^ (2 * k)) for i in range(groups)])
            for k in range(1, chips)
        ]
        return call(finish_kernel, array(4, rows, width), [VMEM] * chips, 1_000_000)(*[pieces[k] for k in finish_order(chips)])

    partial_value = call(
        functools.partial(shade_kernel, lambda i: i), array(tiles, 4, rows, LANES), [VMEM] * 6, 4_000_000
    )(*lit)
    natural = partial_value.transpose(1, 2, 0, 3).reshape(4, rows, groups, width)
    pieces = lax.all_to_all(
        natural.transpose(2, 0, 1, 3), "depth", split_axis=0, concat_axis=0, tiled=True
    )
    while pieces.shape[0] > 1:
        pieces = composite_over(pieces[0::2], pieces[1::2])
    finished = pieces[0]
    return jnp.concatenate([finished[:3], 1.0 - finished[3:]], axis=0)


def solution(mesh):
    placed = (
        P("depth", "strip", None),
        P("depth", "strip", None),
        P("depth", "strip", None),
        P(),
        P(),
    )
    return jax.shard_map(
        on_device, mesh=mesh, in_specs=placed, out_specs=P(None, "strip", "depth"), check_vma=False
    )
```

```python
import functools

import jax
import jax.numpy as jnp
from jax import lax
from jax.experimental import pallas as pl
from jax.experimental.pallas import tpu as pltpu
from jax.sharding import PartitionSpec as P

ambient = 0.3
diffuse = 0.7
LANES = 128
ROWS = 8
VMEM = pl.BlockSpec(memory_space=pltpu.VMEM)


def inner_pairs(count):
    return [(i, i ^ 1) for i in range(count)]


def outer_pairs(groups, strips, axis):
    pairs = []
    for g in range(groups):
        for s in range(strips):
            if axis == "depth":
                to = (g, s ^ 1) if g in (0, groups - 1) else (g + 1 if g % 2 else g - 1, s)
            else:
                to = (g ^ 1, s) if s in (0, strips - 1) else (g, s + 1 if s % 2 else s - 1)
            pairs.append((g * strips + s, to[0] * strips + to[1]))
    return pairs


def tile(c):
    return pl.ds(pl.multiple_of(c * LANES, LANES), LANES)


def call(kernel, out_shape, args, after=()):
    count = len(args)

    def body(*refs):
        kernel(*refs[:count], *refs[count + len(after) :])

    return pl.pallas_call(
        body,
        out_shape=out_shape,
        in_specs=[VMEM] * count + [pl.BlockSpec(memory_space=pl.ANY)] * len(after),
        out_specs=jax.tree.map(lambda _: VMEM, out_shape),
        cost_estimate=pl.CostEstimate(flops=2_000_000, bytes_accessed=2_000_000, transcendentals=0),
        compiler_params=pltpu.CompilerParams(vmem_limit_bytes=16 * 1024 * 1024),
    )(*args, *after)


def array(*shape):
    return jax.ShapeDtypeStruct(shape, jnp.float32)


def load_kernel(order, *refs):
    density, materials, flags, tf_color, tf_opacity = refs[:5]
    brick, held_materials, held_color, held_opacity, layer, inner_y, outer_y, held_flags, sems = refs[5:]
    slices, rows, columns = density.shape
    pairs = (
        (density, brick.at[:, :, pl.ds(0, columns)]),
        (materials, held_materials),
        (flags, held_flags),
        (tf_color, held_color),
        (tf_opacity, held_opacity),
    )
    copies = [pltpu.make_async_copy(x, y, sems.at[i]) for i, (x, y) in enumerate(pairs)]
    for copy in copies:
        copy.start()
    odd_z = lax.axis_index("depth") % 2
    odd_y = lax.axis_index("strip") % 2 == 1
    copies[0].wait()
    layer[0] = brick[(slices - 1) * odd_z, :, :columns]
    for z in range(slices):
        first, last = brick[z, :1, :columns], brick[z, rows - 1 :, :columns]
        inner_y[z : z + 1, :] = jnp.where(odd_y, first, last)
        outer_y[z : z + 1, :] = jnp.where(odd_y, last, first)
    for copy in copies[1:]:
        copy.wait()
    half = columns // LANES // 2
    for i in range(half):
        given = held_materials[:, :, tile(order(1, i))].astype(jnp.float32)
        brick[:, :, columns + i * LANES : columns + (i + 1) * LANES] = given
    occupied = [held_flags[:, :].astype(jnp.float32)] * (LANES // flags.shape[1])
    occupied = jnp.concatenate(occupied, axis=1)
    brick[0, :ROWS, columns + half * LANES :] = jnp.broadcast_to(occupied, (ROWS, LANES))


def by_lane(table):
    here = [table[m : m + 1, :] for m in range(table.shape[0])]
    last = table.shape[1] - 1
    further = [jnp.concatenate([t[:, 1:], t[:, last:]], axis=1) for t in here]
    return jnp.concatenate(here + here, axis=1), jnp.concatenate(further + further, axis=1)


def lookup_kernel(order, columns, start, brick, tf_color, tf_opacity, *refs):
    materials, out = refs if len(refs) == 2 else (None, refs[0])
    slices, rows = brick.shape[:2]
    knots = tf_opacity.shape[1]
    lane = lax.broadcasted_iota(jnp.int32, (1, LANES), 1)
    table = []
    for ch in range(3):
        value, further = by_lane(tf_color[ch])
        low = (further * 65535.0 + 0.5).astype(jnp.int32)
        high = jnp.floor((value * (32767.0 * 65536.0) - low.astype(jnp.float32)) * (1.0 / 65536.0) + 0.5)
        table.append(jnp.broadcast_to(high.astype(jnp.int32) * 65536 + low, (ROWS, LANES)))
    value, further = by_lane(tf_opacity[...])
    rates = jnp.broadcast_to(jnp.where(lane < LANES // 2, value, further - value), (ROWS, LANES))

    occupied = brick[0, :ROWS, columns + columns // 2 :]

    def look(t, index):
        return jnp.take_along_axis(t, index, axis=1, mode="promise_in_bounds")

    def body(at, _):
        i = start + at
        c = order(0, i)
        here = tile(c)
        present = look(occupied, jnp.full((ROWS, LANES), c, jnp.int32))
        for b in range(rows // ROWS):
            band = slice(b * ROWS, (b + 1) * ROWS)
            transmit = None
            for z in range(slices):
                position = jnp.clip(
                    (brick[z, band, here] + 3.0) * ((knots - 1) / 6.0), 0.0, knots - 1.0
                )
                whole = position.astype(jnp.int32)
                part = position - whole.astype(jnp.float32)
                if materials is None:
                    material = brick[z, band, tile(columns // LANES + i)].astype(jnp.int32)
                else:
                    material = materials[z, band, here]
                index = material * knots + whole
                rate = look(rates, index) + part * look(rates, index + LANES // 2)
                clear = jnp.exp(-(rate * present))
                weight = 1.0 - clear
                if z:
                    weight = weight * transmit
                of_low = (part * weight) * (1.0 / 65535.0)
                of_high = (weight - part * weight) * (1.0 / (32767.0 * 65536.0))
                for ch in range(3):
                    both = look(table[ch], index)
                    low = (both & 65535).astype(jnp.float32)
                    out[at, z * 3 + ch, band, :] = both.astype(jnp.float32) * of_high + low * of_low
                transmit = transmit * clear if z else clear
            out[at, slices * 3, band, :] = transmit
        return 0

    lax.fori_loop(0, out.shape[0], body, 0, unroll=out.shape[0])


def over(swap, nearer, farther):
    first = [jnp.where(swap, f, n) for n, f in zip(nearer, farther)]
    second = [jnp.where(swap, n, f) for n, f in zip(nearer, farther)]
    return [first[ch] + first[3] * second[ch] for ch in range(3)] + [first[3] * second[3]]


def hand_kernel(order, far_z, near_y, far_y, out):
    _, rows, _ = far_z.shape
    slices = near_y.shape[0]
    for i in range(out.shape[0]):
        here = tile(order(1, i))
        out[i, :rows, :] = far_z[0, :, here]
        out[i, rows : rows + slices, :] = near_y[:, here]
        out[i, rows + slices :, :] = far_y[:, here]


def shade(order, columns, start, outs, brick, beside, weights, layer, near_row, far_row, odd_slab, finish):
    slices, rows = brick.shape[:2]
    tiles, bands = columns // LANES, rows // ROWS
    lane = lax.broadcasted_iota(jnp.int32, (ROWS, LANES), 1)
    row = lax.broadcasted_iota(jnp.int32, (ROWS, LANES), 0)
    chip, chips = lax.axis_index("depth") // 2, lax.axis_size("depth") // 2
    at_y = lax.axis_index("strip")
    odd_y = at_y % 2 == 1
    has_nearer = jnp.where(chip > 0, 1.0, 0.0)
    has_farther = jnp.where(chip < chips - 1, 1.0, 0.0)
    has_top = jnp.where(at_y > 0, 1.0, 0.0)
    has_bottom = jnp.where(at_y < lax.axis_size("strip") - 1, 1.0, 0.0)
    facing_layer = jnp.where(odd_slab, slices - 1, 0)
    work = [(out, h) for out in outs for h in range(out.shape[0])]
    for i, (out, h) in enumerate(work, start):
        c = order(0, i)
        here, left, right = tile(c), tile(jnp.maximum(c - 1, 0)), tile(jnp.minimum(c + 1, tiles - 1))
        has_left = jnp.where(c > 0, 1.0, 0.0)
        has_right = jnp.where(c < tiles - 1, 1.0, 0.0)
        d = [[brick[z, b * ROWS : (b + 1) * ROWS, here] for b in range(bands)] for z in range(slices)]
        for b in range(bands):
            band = slice(b * ROWS, (b + 1) * ROWS)
            radiance = [None] * 3
            for z in range(slices):
                v = d[z][b]
                if z == 0:
                    nearer = jnp.where(odd_slab, beside[facing_layer, band, here], layer(i, c, band) * has_nearer)
                else:
                    nearer = d[z - 1][b]
                if z == slices - 1:
                    farther = jnp.where(odd_slab, layer(i, c, band) * has_farther, beside[facing_layer, band, here])
                else:
                    farther = d[z + 1][b]
                dz = farther - nearer
                if b == 0:
                    top = jnp.where(odd_y, near_row(i, c, z), far_row(i, c, z))
                    top = jnp.broadcast_to(top * has_top, (ROWS, LANES))
                else:
                    top = d[z][b - 1]
                if b == bands - 1:
                    bottom = jnp.where(odd_y, far_row(i, c, z), near_row(i, c, z))
                    bottom = jnp.broadcast_to(bottom * has_bottom, (ROWS, LANES))
                else:
                    bottom = d[z][b + 1]
                dy = pltpu.roll(jnp.where(row == 0, bottom, v), ROWS - 1, 0) - pltpu.roll(
                    jnp.where(row == ROWS - 1, top, v), 1, 0
                )
                vl = brick[z, band, left] * has_left
                vr = brick[z, band, right] * has_right
                dx = pltpu.roll(jnp.where(lane == 0, vr, v), LANES - 1, 1) - pltpu.roll(
                    jnp.where(lane == LANES - 1, vl, v), 1, 1
                )
                facing = jnp.abs(dx + 2.0 * (dy + dz))
                lighting = ambient + (diffuse / 3.0) * facing * lax.rsqrt(
                    4.0 + (dx * dx + dy * dy + dz * dz)
                )
                for ch in range(3):
                    term = weights[i - start, z * 3 + ch, band, :] * lighting
                    radiance[ch] = radiance[ch] + term if z else term
            image = finish(i - start, band, radiance + [weights[i - start, slices * 3, band, :]])
            for ch in range(4):
                out[h, ch, band, :] = image[ch]


def own_kernel(order, columns, start, brick, beside, weights, far_z, near_y, far_y, out):
    shade(
        order,
        columns,
        start,
        [out],
        brick,
        beside,
        weights,
        lambda i, c, band: far_z[0, band, tile(c)],
        lambda i, c, z: near_y[z : z + 1, tile(c)],
        lambda i, c, z: far_y[z : z + 1, tile(c)],
        lax.axis_index("depth") % 2 == 1,
        lambda i, band, image: image,
    )


def chip_kernel(order, columns, start, brick, beside, weights, handed, mine, *outs):
    slices, rows = brick.shape[:2]
    odd = lax.axis_index("depth") % 2 == 1
    shade(
        order,
        columns,
        start,
        outs,
        brick,
        beside,
        weights,
        lambda i, c, band: handed[i, band, :],
        lambda i, c, z: handed[i, rows + z : rows + z + 1, :],
        lambda i, c, z: handed[i, rows + slices + z : rows + slices + z + 1, :],
        lax.axis_index("depth") % 2 == 0,
        lambda i, band, image: over(odd, [mine[i, ch, band, :] for ch in range(4)], image),
    )


def chip_order(chips):
    return sorted(range(chips), key=lambda k: (-k.bit_count(), k))


def finish_kernel(*refs):
    given, out = dict(zip(chip_order(len(refs) - 1), refs)), refs[-1]
    pieces = [given[k] for k in range(len(given))]
    chip = lax.axis_index("depth") // 2
    for h in range(pieces[0].shape[0]):
        values = [[piece[h, ch] for ch in range(4)] for piece in pieces]
        bit = 0
        while len(values) > 1:
            swap = (chip >> bit) % 2 == 1
            values = [over(swap, values[k], values[k + 1]) for k in range(0, len(values), 2)]
            bit += 1
        here = slice(h * LANES, (h + 1) * LANES)
        for ch in range(3):
            out[ch, :, here] = values[0][ch]
        out[3, :, here] = 1.0 - values[0][3]


def composite_over(nearer, farther):
    return jnp.concatenate(
        [nearer[:, :3] + nearer[:, 3:] * farther[:, :3], nearer[:, 3:] * farther[:, 3:]], axis=1
    )


def on_device(density, materials, occupancy_flags, tf_color, tf_opacity):
    slices, rows, columns = density.shape
    tiles = columns // LANES
    groups, strips = lax.axis_size("depth"), lax.axis_size("strip")
    width = columns // groups
    chips, half = groups // 2, tiles // 2
    paired = chips & (chips - 1) == 0 and width % LANES == 0
    per = width // LANES if paired else half
    ks = chip_order(chips) if paired else [0]

    def order(other, i):
        index = lax.axis_index("depth")
        parity = (index + other) % 2
        if not paired:
            return parity * half + i
        k = sum(jnp.where(i // per == n, ks[n], 0) for n in range(chips))
        return ((index // 2 ^ k) * 2 + parity) * per + i % per

    given = (density, materials, occupancy_flags[0], tf_color.transpose(1, 0, 2), tf_opacity)
    whole = array(slices, rows, columns + half * LANES + LANES)
    edge = array(slices, columns)
    brick, materials, tf_color, tf_opacity, layer, inner_y, outer_y = pl.pallas_call(
        functools.partial(load_kernel, order),
        out_shape=[whole]
        + [jax.ShapeDtypeStruct(given[n].shape, given[n].dtype) for n in (1, 3, 4)]
        + [array(1, rows, columns), edge, edge],
        in_specs=[pl.BlockSpec(memory_space=pltpu.HBM)] * 5,
        out_specs=[VMEM] * 7,
        scratch_shapes=[pltpu.VMEM(given[2].shape, jnp.int32), pltpu.SemaphoreType.DMA((5,))],
        compiler_params=pltpu.CompilerParams(vmem_limit_bytes=16 * 1024 * 1024),
    )(*[pltpu.with_memory_space_constraint(x, pltpu.HBM) for x in given])
    both = ("depth", "strip")
    beside = lax.ppermute(brick, "depth", inner_pairs(groups))
    far_z = lax.ppermute(layer, both, outer_pairs(groups, strips, "depth"))
    near_y = lax.ppermute(inner_y, "strip", inner_pairs(strips))
    far_y = lax.ppermute(outer_y, both, outer_pairs(groups, strips, "strip"))

    far = (chips - 1) * per if paired else half

    def weigh(first, count, after=()):
        lookup = functools.partial(lookup_kernel, order, columns, first)
        shape = array(count, slices * 3 + 1, rows, LANES)
        mine = call(lookup, shape, (brick, tf_color, tf_opacity, materials), after)
        return mine, call(lookup, shape, (beside, tf_color, tf_opacity), (mine,))

    weights, weights_beside = weigh(0, far)
    handing = call(
        functools.partial(hand_kernel, order),
        array(half, rows + 2 * slices, LANES),
        (far_z, near_y, far_y),
        (weights_beside,),
    )
    handed = lax.ppermute(handing, "depth", inner_pairs(groups))

    def images(first, count, blocks, weights, weights_beside):
        mine = call(
            functools.partial(own_kernel, order, columns, first),
            array(count, 4, rows, LANES),
            (brick, beside, weights, far_z, near_y, far_y),
        )
        return call(
            functools.partial(chip_kernel, order, columns, first),
            [array(count // blocks, 4, rows, LANES)] * blocks,
            (beside, brick, weights_beside, handed, mine),
        )

    if paired:
        sent = images(0, far, chips - 1, weights, weights_beside)
        moved = [
            lax.ppermute(image, "depth", [(i, i ^ (2 * k)) for i in range(groups)])
            for image, k in zip(sent, ks)
        ]
        (kept,) = images(far, per, 1, *weigh(far, per, sent[-1:]))
        return call(finish_kernel, array(4, rows, width), (*moved, kept))

    (image,) = images(0, half, 1, weights, weights_beside)
    clear = jnp.zeros_like(image).at[:, 3].set(1.0)
    odd = lax.axis_index("depth") % 2 == 1
    partial_value = jnp.concatenate(
        [jnp.where(odd, clear, image), jnp.where(odd, image, clear)], axis=0
    )
    natural = partial_value.transpose(1, 2, 0, 3).reshape(4, rows, groups, width)
    pieces = lax.all_to_all(
        natural.transpose(2, 0, 1, 3), "depth", split_axis=0, concat_axis=0, tiled=True
    )
    while pieces.shape[0] > 1:
        pieces = composite_over(pieces[0::2], pieces[1::2])
    finished = pieces[0]
    return jnp.concatenate([finished[:3], 1.0 - finished[3:]], axis=0)


def solution(mesh):
    placed = (
        P("depth", "strip", None),
        P("depth", "strip", None),
        P("depth", "strip", None),
        P(),
        P(),
    )
    return jax.shard_map(
        on_device, mesh=mesh, in_specs=placed, out_specs=P(None, "strip", "depth"), check_vma=False
    )
```

```python
import functools

import jax
import jax.numpy as jnp
from jax import lax
from jax.experimental import pallas as pl
from jax.experimental.pallas import tpu as pltpu
from jax.sharding import PartitionSpec as P

ambient = 0.3
diffuse = 0.7
LANES = 128
ROWS = 8
VMEM = pl.BlockSpec(memory_space=pltpu.VMEM)


def inner_pairs(count):
    return [(i, i ^ 1) for i in range(count)]


def outer_pairs(groups, strips, axis):
    pairs = []
    for g in range(groups):
        for s in range(strips):
            if axis == "depth":
                to = (g, s ^ 1) if g in (0, groups - 1) else (g + 1 if g % 2 else g - 1, s)
            else:
                to = (g ^ 1, s) if s in (0, strips - 1) else (g, s + 1 if s % 2 else s - 1)
            pairs.append((g * strips + s, to[0] * strips + to[1]))
    return pairs


def tile(c):
    return pl.ds(pl.multiple_of(c * LANES, LANES), LANES)


def call(kernel, out_shape, args, after=()):
    count = len(args)

    def body(*refs):
        kernel(*refs[:count], *refs[count + len(after) :])

    return pl.pallas_call(
        body,
        out_shape=out_shape,
        in_specs=[VMEM] * count + [pl.BlockSpec(memory_space=pl.ANY)] * len(after),
        out_specs=jax.tree.map(lambda _: VMEM, out_shape),
        cost_estimate=pl.CostEstimate(flops=2_000_000, bytes_accessed=2_000_000, transcendentals=0),
        compiler_params=pltpu.CompilerParams(vmem_limit_bytes=16 * 1024 * 1024),
    )(*args, *after)


def array(*shape):
    return jax.ShapeDtypeStruct(shape, jnp.float32)


def load_kernel(order, *refs):
    density, materials, flags, tf_color, tf_opacity = refs[:5]
    brick, held_materials, held_color, held_opacity, layer, inner_y, outer_y, held_flags, sems = refs[5:]
    slices, rows, columns = density.shape
    pairs = (
        (density, brick.at[:, :, pl.ds(0, columns)]),
        (materials, held_materials),
        (flags, held_flags),
        (tf_color, held_color),
        (tf_opacity, held_opacity),
    )
    copies = [pltpu.make_async_copy(x, y, sems.at[i]) for i, (x, y) in enumerate(pairs)]
    for copy in copies[1:] + copies[:1]:
        copy.start()
    odd_z = lax.axis_index("depth") % 2
    odd_y = lax.axis_index("strip") % 2 == 1
    for copy in copies[1:]:
        copy.wait()
    half = columns // LANES // 2
    for i in range(half):
        given = held_materials[:, :, tile(order(1, i))].astype(jnp.float32)
        brick[:, :, columns + i * LANES : columns + (i + 1) * LANES] = given
    occupied = [held_flags[:, :].astype(jnp.float32)] * (LANES // flags.shape[1])
    occupied = jnp.concatenate(occupied, axis=1)
    brick[0, :ROWS, columns + half * LANES :] = jnp.broadcast_to(occupied, (ROWS, LANES))
    copies[0].wait()
    layer[0] = brick[(slices - 1) * odd_z, :, :columns]
    for z in range(slices):
        first, last = brick[z, :1, :columns], brick[z, rows - 1 :, :columns]
        inner_y[z : z + 1, :] = jnp.where(odd_y, first, last)
        outer_y[z : z + 1, :] = jnp.where(odd_y, last, first)


def by_lane(table):
    here = [table[m : m + 1, :] for m in range(table.shape[0])]
    last = table.shape[1] - 1
    further = [jnp.concatenate([t[:, 1:], t[:, last:]], axis=1) for t in here]
    return jnp.concatenate(here + here, axis=1), jnp.concatenate(further + further, axis=1)


def lookup_kernel(order, columns, start, brick, tf_color, tf_opacity, *refs):
    materials, out = refs if len(refs) == 2 else (None, refs[0])
    slices, rows = brick.shape[:2]
    knots = tf_opacity.shape[1]
    lane = lax.broadcasted_iota(jnp.int32, (1, LANES), 1)
    table = []
    for ch in range(3):
        value, further = by_lane(tf_color[ch])
        low = (further * 65535.0 + 0.5).astype(jnp.int32)
        high = jnp.floor((value * (32767.0 * 65536.0) - low.astype(jnp.float32)) * (1.0 / 65536.0) + 0.5)
        table.append(jnp.broadcast_to(high.astype(jnp.int32) * 65536 + low, (ROWS, LANES)))
    value, further = by_lane(tf_opacity[...])
    rates = jnp.broadcast_to(jnp.where(lane < LANES // 2, value, further - value), (ROWS, LANES))

    occupied = brick[0, :ROWS, columns + columns // 2 :]

    def look(t, index):
        return jnp.take_along_axis(t, index, axis=1, mode="promise_in_bounds")

    def body(at, _):
        i = start + at
        c = order(0, i)
        here = tile(c)
        present = look(occupied, jnp.full((ROWS, LANES), c, jnp.int32))
        for b in range(rows // ROWS):
            band = slice(b * ROWS, (b + 1) * ROWS)
            transmit = None
            for z in range(slices):
                position = jnp.clip(
                    (brick[z, band, here] + 3.0) * ((knots - 1) / 6.0), 0.0, knots - 1.0
                )
                whole = position.astype(jnp.int32)
                part = position - whole.astype(jnp.float32)
                if materials is None:
                    material = brick[z, band, tile(columns // LANES + i)].astype(jnp.int32)
                else:
                    material = materials[z, band, here]
                index = material * knots + whole
                rate = look(rates, index) + part * look(rates, index + LANES // 2)
                clear = jnp.exp(-(rate * present))
                weight = 1.0 - clear
                if z:
                    weight = weight * transmit
                of_low = (part * weight) * (1.0 / 65535.0)
                of_high = (weight - part * weight) * (1.0 / (32767.0 * 65536.0))
                for ch in range(3):
                    both = look(table[ch], index)
                    low = (both & 65535).astype(jnp.float32)
                    out[at, z * 3 + ch, band, :] = both.astype(jnp.float32) * of_high + low * of_low
                transmit = transmit * clear if z else clear
            out[at, slices * 3, band, :] = transmit
        return 0

    lax.fori_loop(0, out.shape[0], body, 0, unroll=out.shape[0])


def over(swap, nearer, farther):
    first = [jnp.where(swap, f, n) for n, f in zip(nearer, farther)]
    second = [jnp.where(swap, n, f) for n, f in zip(nearer, farther)]
    return [first[ch] + first[3] * second[ch] for ch in range(3)] + [first[3] * second[3]]


def hand_kernel(order, start, far_z, near_y, far_y, out):
    _, rows, _ = far_z.shape
    slices = near_y.shape[0]
    for i in range(out.shape[0]):
        here = tile(order(1, start + i))
        out[i, :rows, :] = far_z[0, :, here]
        out[i, rows : rows + slices, :] = near_y[:, here]
        out[i, rows + slices :, :] = far_y[:, here]


def shade(order, columns, start, outs, brick, beside, weights, layer, near_row, far_row, odd_slab, finish):
    slices, rows = brick.shape[:2]
    tiles, bands = columns // LANES, rows // ROWS
    lane = lax.broadcasted_iota(jnp.int32, (ROWS, LANES), 1)
    row = lax.broadcasted_iota(jnp.int32, (ROWS, LANES), 0)
    chip, chips = lax.axis_index("depth") // 2, lax.axis_size("depth") // 2
    at_y = lax.axis_index("strip")
    odd_y = at_y % 2 == 1
    has_nearer = jnp.where(chip > 0, 1.0, 0.0)
    has_farther = jnp.where(chip < chips - 1, 1.0, 0.0)
    has_top = jnp.where(at_y > 0, 1.0, 0.0)
    has_bottom = jnp.where(at_y < lax.axis_size("strip") - 1, 1.0, 0.0)
    facing_layer = jnp.where(odd_slab, slices - 1, 0)
    work = [(out, h) for out in outs for h in range(out.shape[0])]
    for i, (out, h) in enumerate(work, start):
        c = order(0, i)
        here, left, right = tile(c), tile(jnp.maximum(c - 1, 0)), tile(jnp.minimum(c + 1, tiles - 1))
        has_left = jnp.where(c > 0, 1.0, 0.0)
        has_right = jnp.where(c < tiles - 1, 1.0, 0.0)
        d = [[brick[z, b * ROWS : (b + 1) * ROWS, here] for b in range(bands)] for z in range(slices)]
        for b in range(bands):
            band = slice(b * ROWS, (b + 1) * ROWS)
            radiance = [None] * 3
            for z in range(slices):
                v = d[z][b]
                if z == 0:
                    nearer = jnp.where(odd_slab, beside[facing_layer, band, here], layer(i, c, band) * has_nearer)
                else:
                    nearer = d[z - 1][b]
                if z == slices - 1:
                    farther = jnp.where(odd_slab, layer(i, c, band) * has_farther, beside[facing_layer, band, here])
                else:
                    farther = d[z + 1][b]
                dz = farther - nearer
                if b == 0:
                    top = jnp.where(odd_y, near_row(i, c, z), far_row(i, c, z))
                    top = jnp.broadcast_to(top * has_top, (ROWS, LANES))
                else:
                    top = d[z][b - 1]
                if b == bands - 1:
                    bottom = jnp.where(odd_y, far_row(i, c, z), near_row(i, c, z))
                    bottom = jnp.broadcast_to(bottom * has_bottom, (ROWS, LANES))
                else:
                    bottom = d[z][b + 1]
                dy = pltpu.roll(jnp.where(row == 0, bottom, v), ROWS - 1, 0) - pltpu.roll(
                    jnp.where(row == ROWS - 1, top, v), 1, 0
                )
                vl = brick[z, band, left] * has_left
                vr = brick[z, band, right] * has_right
                dx = pltpu.roll(jnp.where(lane == 0, vr, v), LANES - 1, 1) - pltpu.roll(
                    jnp.where(lane == LANES - 1, vl, v), 1, 1
                )
                facing = jnp.abs(dx + 2.0 * (dy + dz))
                lighting = ambient + (diffuse / 3.0) * facing * lax.rsqrt(
                    4.0 + (dx * dx + dy * dy + dz * dz)
                )
                for ch in range(3):
                    term = weights[i - start, z * 3 + ch, band, :] * lighting
                    radiance[ch] = radiance[ch] + term if z else term
            image = finish(i - start, band, radiance + [weights[i - start, slices * 3, band, :]])
            for ch in range(4):
                out[h, ch, band, :] = image[ch]


def own_kernel(order, columns, start, brick, beside, weights, far_z, near_y, far_y, out):
    shade(
        order,
        columns,
        start,
        [out],
        brick,
        beside,
        weights,
        lambda i, c, band: far_z[0, band, tile(c)],
        lambda i, c, z: near_y[z : z + 1, tile(c)],
        lambda i, c, z: far_y[z : z + 1, tile(c)],
        lax.axis_index("depth") % 2 == 1,
        lambda i, band, image: image,
    )


def chip_kernel(order, columns, start, brick, beside, weights, handed, mine, *outs):
    slices, rows = brick.shape[:2]
    odd = lax.axis_index("depth") % 2 == 1
    shade(
        order,
        columns,
        start,
        outs,
        brick,
        beside,
        weights,
        lambda i, c, band: handed[i - start, band, :],
        lambda i, c, z: handed[i - start, rows + z : rows + z + 1, :],
        lambda i, c, z: handed[i - start, rows + slices + z : rows + slices + z + 1, :],
        lax.axis_index("depth") % 2 == 0,
        lambda i, band, image: over(odd, [mine[i, ch, band, :] for ch in range(4)], image),
    )


def chip_order(chips):
    return sorted(range(chips), key=lambda k: (-k.bit_count(), k))


def finish_kernel(*refs):
    given, out = dict(zip(chip_order(len(refs) - 1), refs)), refs[-1]
    pieces = [given[k] for k in range(len(given))]
    chip = lax.axis_index("depth") // 2
    for h in range(pieces[0].shape[0]):
        values = [[piece[h, ch] for ch in range(4)] for piece in pieces]
        bit = 0
        while len(values) > 1:
            swap = (chip >> bit) % 2 == 1
            values = [over(swap, values[k], values[k + 1]) for k in range(0, len(values), 2)]
            bit += 1
        here = slice(h * LANES, (h + 1) * LANES)
        for ch in range(3):
            out[ch, :, here] = values[0][ch]
        out[3, :, here] = 1.0 - values[0][3]


def composite_over(nearer, farther):
    return jnp.concatenate(
        [nearer[:, :3] + nearer[:, 3:] * farther[:, :3], nearer[:, 3:] * farther[:, 3:]], axis=1
    )


def on_device(density, materials, occupancy_flags, tf_color, tf_opacity):
    slices, rows, columns = density.shape
    tiles = columns // LANES
    groups, strips = lax.axis_size("depth"), lax.axis_size("strip")
    width = columns // groups
    chips, half = groups // 2, tiles // 2
    paired = chips & (chips - 1) == 0 and width % LANES == 0
    per = width // LANES if paired else half
    ks = chip_order(chips) if paired else [0]

    def order(other, i):
        index = lax.axis_index("depth")
        parity = (index + other) % 2
        if not paired:
            return parity * half + i
        k = sum(jnp.where(i // per == n, ks[n], 0) for n in range(chips))
        return ((index // 2 ^ k) * 2 + parity) * per + i % per

    given = (density, materials, occupancy_flags[0], tf_color.transpose(1, 0, 2), tf_opacity)
    whole = array(slices, rows, columns + half * LANES + LANES)
    edge = array(slices, columns)
    brick, materials, tf_color, tf_opacity, layer, inner_y, outer_y = pl.pallas_call(
        functools.partial(load_kernel, order),
        out_shape=[whole]
        + [jax.ShapeDtypeStruct(given[n].shape, given[n].dtype) for n in (1, 3, 4)]
        + [array(1, rows, columns), edge, edge],
        in_specs=[pl.BlockSpec(memory_space=pltpu.HBM)] * 5,
        out_specs=[VMEM] * 7,
        scratch_shapes=[pltpu.VMEM(given[2].shape, jnp.int32), pltpu.SemaphoreType.DMA((5,))],
        compiler_params=pltpu.CompilerParams(vmem_limit_bytes=16 * 1024 * 1024),
    )(*[pltpu.with_memory_space_constraint(x, pltpu.HBM) for x in given])
    both = ("depth", "strip")
    beside = lax.ppermute(brick, "depth", inner_pairs(groups))
    far_z = lax.ppermute(layer, both, outer_pairs(groups, strips, "depth"))
    near_y = lax.ppermute(inner_y, "strip", inner_pairs(strips))
    far_y = lax.ppermute(outer_y, both, outer_pairs(groups, strips, "strip"))

    far = (chips - 1) * per if paired else half

    def weigh(first, count, after=()):
        lookup = functools.partial(lookup_kernel, order, columns, first)
        shape = array(count, slices * 3 + 1, rows, LANES)
        mine = call(lookup, shape, (brick, tf_color, tf_opacity, materials), after)
        return mine, call(lookup, shape, (beside, tf_color, tf_opacity), (mine,))

    weights, weights_beside = weigh(0, far)
    def hand(first, count, after):
        handing = call(
            functools.partial(hand_kernel, order, first),
            array(count, rows + 2 * slices, LANES),
            (far_z, near_y, far_y),
            after,
        )
        return lax.ppermute(handing, "depth", inner_pairs(groups))

    handed = hand(0, far, (weights_beside,))

    def images(first, count, blocks, handed, weights, weights_beside):
        mine = call(
            functools.partial(own_kernel, order, columns, first),
            array(count, 4, rows, LANES),
            (brick, beside, weights, far_z, near_y, far_y),
        )
        return call(
            functools.partial(chip_kernel, order, columns, first),
            [array(count // blocks, 4, rows, LANES)] * blocks,
            (beside, brick, weights_beside, handed, mine),
        )

    if paired:
        sent = images(0, far, chips - 1, handed, weights, weights_beside)
        moved = [
            lax.ppermute(image, "depth", [(i, i ^ (2 * k)) for i in range(groups)])
            for image, k in zip(sent, ks)
        ]
        late = sent[-1:]
        (kept,) = images(far, per, 1, hand(far, per, late), *weigh(far, per, late))
        return call(finish_kernel, array(4, rows, width), (*moved, kept))

    (image,) = images(0, half, 1, handed, weights, weights_beside)
    clear = jnp.zeros_like(image).at[:, 3].set(1.0)
    odd = lax.axis_index("depth") % 2 == 1
    partial_value = jnp.concatenate(
        [jnp.where(odd, clear, image), jnp.where(odd, image, clear)], axis=0
    )
    natural = partial_value.transpose(1, 2, 0, 3).reshape(4, rows, groups, width)
    pieces = lax.all_to_all(
        natural.transpose(2, 0, 1, 3), "depth", split_axis=0, concat_axis=0, tiled=True
    )
    while pieces.shape[0] > 1:
        pieces = composite_over(pieces[0::2], pieces[1::2])
    finished = pieces[0]
    return jnp.concatenate([finished[:3], 1.0 - finished[3:]], axis=0)


def solution(mesh):
    placed = (
        P("depth", "strip", None),
        P("depth", "strip", None),
        P("depth", "strip", None),
        P(),
        P(),
    )
    return jax.shard_map(
        on_device, mesh=mesh, in_specs=placed, out_specs=P(None, "strip", "depth"), check_vma=False
    )
```

```python
import functools

import jax
import jax.numpy as jnp
from jax import lax
from jax.experimental import pallas as pl
from jax.experimental.pallas import tpu as pltpu
from jax.sharding import PartitionSpec as P

ambient = 0.3
diffuse = 0.7
LANES = 128
ROWS = 8
VMEM = pl.BlockSpec(memory_space=pltpu.VMEM)


def inner_pairs(count):
    return [(i, i ^ 1) for i in range(count)]


def outer_pairs(groups, strips, axis):
    pairs = []
    for g in range(groups):
        for s in range(strips):
            if axis == "depth":
                to = (g, s ^ 1) if g in (0, groups - 1) else (g + 1 if g % 2 else g - 1, s)
            else:
                to = (g ^ 1, s) if s in (0, strips - 1) else (g, s + 1 if s % 2 else s - 1)
            pairs.append((g * strips + s, to[0] * strips + to[1]))
    return pairs


def tile(c):
    return pl.ds(pl.multiple_of(c * LANES, LANES), LANES)


def call(kernel, out_shape, args, after=()):
    count = len(args)

    def body(*refs):
        kernel(*refs[:count], *refs[count + len(after) :])

    return pl.pallas_call(
        body,
        out_shape=out_shape,
        in_specs=[VMEM] * count + [pl.BlockSpec(memory_space=pl.ANY)] * len(after),
        out_specs=jax.tree.map(lambda _: VMEM, out_shape),
        cost_estimate=pl.CostEstimate(flops=2_000_000, bytes_accessed=2_000_000, transcendentals=0),
        compiler_params=pltpu.CompilerParams(vmem_limit_bytes=16 * 1024 * 1024),
    )(*args, *after)


def array(*shape):
    return jax.ShapeDtypeStruct(shape, jnp.float32)


def load_kernel(order, *refs):
    density, materials, flags, tf_color, tf_opacity = refs[:5]
    brick, held_materials, held_color, held_opacity, layer, inner_y, outer_y, held_flags, sems = refs[5:]
    slices, rows, columns = density.shape
    pairs = (
        (density, brick.at[:, :, pl.ds(0, columns)]),
        (materials, held_materials),
        (flags, held_flags),
        (tf_color, held_color),
        (tf_opacity, held_opacity),
    )
    copies = [pltpu.make_async_copy(x, y, sems.at[i]) for i, (x, y) in enumerate(pairs)]
    for copy in copies[1:] + copies[:1]:
        copy.start()
    odd_z = lax.axis_index("depth") % 2
    odd_y = lax.axis_index("strip") % 2 == 1
    for copy in copies[1:]:
        copy.wait()
    half = columns // LANES // 2
    for i in range(half):
        given = held_materials[:, :, tile(order(1, i))].astype(jnp.float32)
        brick[:, :, columns + i * LANES : columns + (i + 1) * LANES] = given
    occupied = [held_flags[:, :].astype(jnp.float32)] * (LANES // flags.shape[1])
    occupied = jnp.concatenate(occupied, axis=1)
    brick[0, :ROWS, columns + half * LANES :] = jnp.broadcast_to(occupied, (ROWS, LANES))
    copies[0].wait()
    layer[0] = brick[(slices - 1) * odd_z, :, :columns]
    for z in range(slices):
        first, last = brick[z, :1, :columns], brick[z, rows - 1 :, :columns]
        inner_y[z : z + 1, :] = jnp.where(odd_y, first, last)
        outer_y[z : z + 1, :] = jnp.where(odd_y, last, first)


def by_lane(table):
    here = [table[m : m + 1, :] for m in range(table.shape[0])]
    last = table.shape[1] - 1
    further = [jnp.concatenate([t[:, 1:], t[:, last:]], axis=1) for t in here]
    return jnp.concatenate(here + here, axis=1), jnp.concatenate(further + further, axis=1)


def lookup_kernel(order, columns, start, brick, tf_color, tf_opacity, *refs):
    materials, out = refs if len(refs) == 2 else (None, refs[0])
    slices, rows = brick.shape[:2]
    knots = tf_opacity.shape[1]
    lane = lax.broadcasted_iota(jnp.int32, (1, LANES), 1)
    table = []
    for ch in range(3):
        value, further = by_lane(tf_color[ch])
        low = (further * 65535.0 + 0.5).astype(jnp.int32)
        high = jnp.floor((value * (32767.0 * 65536.0) - low.astype(jnp.float32)) * (1.0 / 65536.0) + 0.5)
        table.append(jnp.broadcast_to(high.astype(jnp.int32) * 65536 + low, (ROWS, LANES)))
    value, further = by_lane(tf_opacity[...])
    rates = jnp.broadcast_to(jnp.where(lane < LANES // 2, value, further - value), (ROWS, LANES))

    occupied = brick[0, :ROWS, columns + columns // 2 :]

    def look(t, index):
        return jnp.take_along_axis(t, index, axis=1, mode="promise_in_bounds")

    def body(at, _):
        i = start + at
        c = order(0, i)
        here = tile(c)
        present = look(occupied, jnp.full((ROWS, LANES), c, jnp.int32))
        for b in range(rows // ROWS):
            band = slice(b * ROWS, (b + 1) * ROWS)
            transmit = None
            for z in range(slices):
                position = jnp.clip(
                    (brick[z, band, here] + 3.0) * ((knots - 1) / 6.0), 0.0, knots - 1.0
                )
                whole = position.astype(jnp.int32)
                part = position - whole.astype(jnp.float32)
                if materials is None:
                    material = brick[z, band, tile(columns // LANES + i)].astype(jnp.int32)
                else:
                    material = materials[z, band, here]
                index = material * knots + whole
                rate = look(rates, index) + part * look(rates, index + LANES // 2)
                clear = jnp.exp(-(rate * present))
                weight = 1.0 - clear
                if z:
                    weight = weight * transmit
                of_low = (part * weight) * (1.0 / 65535.0)
                of_high = (weight - part * weight) * (1.0 / (32767.0 * 65536.0))
                for ch in range(3):
                    both = look(table[ch], index)
                    low = (both & 65535).astype(jnp.float32)
                    out[at, z * 3 + ch, band, :] = both.astype(jnp.float32) * of_high + low * of_low
                transmit = transmit * clear if z else clear
            out[at, slices * 3, band, :] = transmit
        return 0

    lax.fori_loop(0, out.shape[0], body, 0, unroll=out.shape[0])


def over(swap, nearer, farther):
    first = [jnp.where(swap, f, n) for n, f in zip(nearer, farther)]
    second = [jnp.where(swap, n, f) for n, f in zip(nearer, farther)]
    return [first[ch] + first[3] * second[ch] for ch in range(3)] + [first[3] * second[3]]


def hand_kernel(order, start, far_z, near_y, far_y, out):
    _, rows, _ = far_z.shape
    slices = near_y.shape[0]
    for i in range(out.shape[0]):
        here = tile(order(1, start + i))
        out[i, :rows, :] = far_z[0, :, here]
        out[i, rows : rows + slices, :] = near_y[:, here]
        out[i, rows + slices :, :] = far_y[:, here]


def column_step(brick, columns, c, z, band, v):
    tiles = columns // LANES
    lane = lax.broadcasted_iota(jnp.int32, (ROWS, LANES), 1)
    vl = brick[z, band, tile(jnp.maximum(c - 1, 0))] * jnp.where(c > 0, 1.0, 0.0)
    vr = brick[z, band, tile(jnp.minimum(c + 1, tiles - 1))] * jnp.where(c < tiles - 1, 1.0, 0.0)
    return pltpu.roll(jnp.where(lane == 0, vr, v), LANES - 1, 1) - pltpu.roll(
        jnp.where(lane == LANES - 1, vl, v), 1, 1
    )


def steps_kernel(order, columns, start, brick, out):
    slices, rows = brick.shape[:2]
    for i in range(out.shape[0]):
        c = order(0, start + i)
        for z in range(slices):
            for b in range(rows // ROWS):
                band = slice(b * ROWS, (b + 1) * ROWS)
                out[i, z, band, :] = column_step(brick, columns, c, z, band, brick[z, band, tile(c)])


def shade(order, columns, start, outs, brick, beside, weights, layer, near_row, far_row, across, odd_slab, finish):
    slices, rows = brick.shape[:2]
    bands = rows // ROWS
    row = lax.broadcasted_iota(jnp.int32, (ROWS, LANES), 0)
    chip, chips = lax.axis_index("depth") // 2, lax.axis_size("depth") // 2
    at_y = lax.axis_index("strip")
    odd_y = at_y % 2 == 1
    has_nearer = jnp.where(chip > 0, 1.0, 0.0)
    has_farther = jnp.where(chip < chips - 1, 1.0, 0.0)
    has_top = jnp.where(at_y > 0, 1.0, 0.0)
    has_bottom = jnp.where(at_y < lax.axis_size("strip") - 1, 1.0, 0.0)
    facing_layer = jnp.where(odd_slab, slices - 1, 0)
    work = [(out, h) for out in outs for h in range(out.shape[0])]
    for i, (out, h) in enumerate(work, start):
        c = order(0, i)
        here = tile(c)
        d = [[brick[z, b * ROWS : (b + 1) * ROWS, here] for b in range(bands)] for z in range(slices)]
        for b in range(bands):
            band = slice(b * ROWS, (b + 1) * ROWS)
            radiance = [None] * 3
            for z in range(slices):
                v = d[z][b]
                if z == 0:
                    nearer = jnp.where(odd_slab, beside[facing_layer, band, here], layer(i, c, band) * has_nearer)
                else:
                    nearer = d[z - 1][b]
                if z == slices - 1:
                    farther = jnp.where(odd_slab, layer(i, c, band) * has_farther, beside[facing_layer, band, here])
                else:
                    farther = d[z + 1][b]
                dz = farther - nearer
                if b == 0:
                    top = jnp.where(odd_y, near_row(i, c, z), far_row(i, c, z))
                    top = jnp.broadcast_to(top * has_top, (ROWS, LANES))
                else:
                    top = d[z][b - 1]
                if b == bands - 1:
                    bottom = jnp.where(odd_y, far_row(i, c, z), near_row(i, c, z))
                    bottom = jnp.broadcast_to(bottom * has_bottom, (ROWS, LANES))
                else:
                    bottom = d[z][b + 1]
                dy = pltpu.roll(jnp.where(row == 0, bottom, v), ROWS - 1, 0) - pltpu.roll(
                    jnp.where(row == ROWS - 1, top, v), 1, 0
                )
                dx = across(i, c, z, band, v)
                facing = jnp.abs(dx + 2.0 * (dy + dz))
                lighting = ambient + (diffuse / 3.0) * facing * lax.rsqrt(
                    4.0 + (dx * dx + dy * dy + dz * dz)
                )
                for ch in range(3):
                    term = weights[i - start, z * 3 + ch, band, :] * lighting
                    radiance[ch] = radiance[ch] + term if z else term
            image = finish(i - start, band, radiance + [weights[i - start, slices * 3, band, :]])
            for ch in range(4):
                out[h, ch, band, :] = image[ch]


def own_kernel(order, columns, start, brick, beside, weights, far_z, near_y, far_y, out):
    shade(
        order,
        columns,
        start,
        [out],
        brick,
        beside,
        weights,
        lambda i, c, band: far_z[0, band, tile(c)],
        lambda i, c, z: near_y[z : z + 1, tile(c)],
        lambda i, c, z: far_y[z : z + 1, tile(c)],
        lambda i, c, z, band, v: column_step(brick, columns, c, z, band, v),
        lax.axis_index("depth") % 2 == 1,
        lambda i, band, image: image,
    )


def chip_kernel(order, columns, start, brick, beside, weights, steps, handed, mine, *outs):
    slices, rows = brick.shape[:2]
    odd = lax.axis_index("depth") % 2 == 1
    shade(
        order,
        columns,
        start,
        outs,
        brick,
        beside,
        weights,
        lambda i, c, band: handed[i, band, :],
        lambda i, c, z: handed[i, rows + z : rows + z + 1, :],
        lambda i, c, z: handed[i, rows + slices + z : rows + slices + z + 1, :],
        lambda i, c, z, band, v: steps[i - start, z, band, :],
        lax.axis_index("depth") % 2 == 0,
        lambda i, band, image: over(odd, [mine[i, ch, band, :] for ch in range(4)], image),
    )


def pass_kernel(received, out):
    per = out.shape[0]
    other = 1 - lax.axis_index("depth") % 2
    for h in range(per):
        out[h] = received[other * per + h]


def finish_kernel(beside, passed, across, mine, out):
    index = lax.axis_index("depth")
    odd, chip = index % 2 == 1, index // 2
    per = mine.shape[0]
    for h in range(per):
        direct = [beside[index % 2 * per + h, ch] for ch in range(4)]
        other = [passed[h, ch] for ch in range(4)]
        along_x = [jnp.where(odd, o, d) for o, d in zip(other, direct)]
        along_y = [jnp.where(odd, d, o) for o, d in zip(other, direct)]
        by_x, by_y = chip % 2 == 1, chip // 2 == 1
        here_row = over(by_x, [mine[h, ch] for ch in range(4)], along_x)
        there_row = over(by_x, along_y, [across[h, ch] for ch in range(4)])
        image = over(by_y, here_row, there_row)
        here = slice(h * LANES, (h + 1) * LANES)
        for ch in range(3):
            out[ch, :, here] = image[ch]
        out[3, :, here] = 1.0 - image[3]


def composite_over(nearer, farther):
    return jnp.concatenate(
        [nearer[:, :3] + nearer[:, 3:] * farther[:, :3], nearer[:, 3:] * farther[:, 3:]], axis=1
    )


def on_device(density, materials, occupancy_flags, tf_color, tf_opacity):
    slices, rows, columns = density.shape
    tiles = columns // LANES
    groups, strips = lax.axis_size("depth"), lax.axis_size("strip")
    width = columns // groups
    chips, half = groups // 2, tiles // 2
    squared = chips == 4 and width % LANES == 0
    per = width // LANES if squared else half

    def order(other, i):
        index = lax.axis_index("depth")
        parity = (index + other) % 2
        if not squared:
            return parity * half + i
        n = i // per
        away = jnp.where(n < 2, 1 + parity, jnp.where(n == 2, 3, 0))
        core = jnp.where(n < 2, n, parity)
        return ((index // 2 ^ away) * 2 + core) * per + i % per

    given = (density, materials, occupancy_flags[0], tf_color.transpose(1, 0, 2), tf_opacity)
    whole = array(slices, rows, columns + half * LANES + LANES)
    edge = array(slices, columns)
    brick, materials, tf_color, tf_opacity, layer, inner_y, outer_y = pl.pallas_call(
        functools.partial(load_kernel, order),
        out_shape=[whole]
        + [jax.ShapeDtypeStruct(given[n].shape, given[n].dtype) for n in (1, 3, 4)]
        + [array(1, rows, columns), edge, edge],
        in_specs=[pl.BlockSpec(memory_space=pltpu.HBM)] * 5,
        out_specs=[VMEM] * 7,
        scratch_shapes=[pltpu.VMEM(given[2].shape, jnp.int32), pltpu.SemaphoreType.DMA((5,))],
        compiler_params=pltpu.CompilerParams(vmem_limit_bytes=16 * 1024 * 1024),
    )(*[pltpu.with_memory_space_constraint(x, pltpu.HBM) for x in given])
    both = ("depth", "strip")
    beside = lax.ppermute(brick, "depth", inner_pairs(groups))
    far_z = lax.ppermute(layer, both, outer_pairs(groups, strips, "depth"))
    near_y = lax.ppermute(inner_y, "strip", inner_pairs(strips))
    far_y = lax.ppermute(outer_y, both, outer_pairs(groups, strips, "strip"))

    far = 3 * per if squared else half

    def weigh(first, count, after=()):
        lookup = functools.partial(lookup_kernel, order, columns, first)
        shape = array(count, slices * 3 + 1, rows, LANES)
        mine = call(lookup, shape, (brick, tf_color, tf_opacity, materials), after)
        return mine, call(lookup, shape, (beside, tf_color, tf_opacity), (mine,))

    weights, weights_beside = weigh(0, far)
    def hand(first, count, after):
        handing = call(
            functools.partial(hand_kernel, order, first),
            array(count, rows + 2 * slices, LANES),
            (far_z, near_y, far_y),
            after,
        )
        return lax.ppermute(handing, "depth", inner_pairs(groups))

    handed = hand(0, half, (weights_beside,))

    def images(first, counts, handed, weights, weights_beside):
        count = sum(counts)
        steps = call(
            functools.partial(steps_kernel, order, columns, first),
            array(count, slices, rows, LANES),
            (beside,),
            (weights_beside,),
        )
        mine = call(
            functools.partial(own_kernel, order, columns, first),
            array(count, 4, rows, LANES),
            (brick, beside, weights, far_z, near_y, far_y),
        )
        return call(
            functools.partial(chip_kernel, order, columns, first),
            [array(tiles_here, 4, rows, LANES) for tiles_here in counts],
            (beside, brick, weights_beside, steps, handed, mine),
        )

    if squared:
        to_side, to_across = images(0, (2 * per, per), handed, weights, weights_beside)
        from_side = lax.ppermute(to_side, "depth", [(i, i ^ 2 << i % 2) for i in range(groups)])
        from_across = lax.ppermute(to_across, "depth", [(i, i ^ 6) for i in range(groups)])
        late = (to_side,)
        (kept,) = images(far, (per,), handed, *weigh(far, per, late))
        (passing,) = call(pass_kernel, [array(per, 4, rows, LANES)], (from_side,), (kept,))
        passed = lax.ppermute(passing, "depth", inner_pairs(groups))
        return call(finish_kernel, array(4, rows, width), (from_side, passed, from_across, kept))

    (image,) = images(0, (half,), handed, weights, weights_beside)
    clear = jnp.zeros_like(image).at[:, 3].set(1.0)
    odd = lax.axis_index("depth") % 2 == 1
    partial_value = jnp.concatenate(
        [jnp.where(odd, clear, image), jnp.where(odd, image, clear)], axis=0
    )
    natural = partial_value.transpose(1, 2, 0, 3).reshape(4, rows, groups, width)
    pieces = lax.all_to_all(
        natural.transpose(2, 0, 1, 3), "depth", split_axis=0, concat_axis=0, tiled=True
    )
    while pieces.shape[0] > 1:
        pieces = composite_over(pieces[0::2], pieces[1::2])
    finished = pieces[0]
    return jnp.concatenate([finished[:3], 1.0 - finished[3:]], axis=0)


def solution(mesh):
    placed = (
        P("depth", "strip", None),
        P("depth", "strip", None),
        P("depth", "strip", None),
        P(),
        P(),
    )
    return jax.shard_map(
        on_device, mesh=mesh, in_specs=placed, out_specs=P(None, "strip", "depth"), check_vma=False
    )
```

```python
import functools

import jax
import jax.numpy as jnp
from jax import lax
from jax.experimental import pallas as pl
from jax.experimental.pallas import tpu as pltpu
from jax.sharding import PartitionSpec as P

ambient = 0.3
diffuse = 0.7
LANES = 128
ROWS = 8
VMEM = pl.BlockSpec(memory_space=pltpu.VMEM)


def inner_pairs(count):
    return [(i, i ^ 1) for i in range(count)]


def outer_pairs(groups, strips, axis):
    pairs = []
    for g in range(groups):
        for s in range(strips):
            if axis == "depth":
                to = (g, s ^ 1) if g in (0, groups - 1) else (g + 1 if g % 2 else g - 1, s)
            else:
                to = (g ^ 1, s) if s in (0, strips - 1) else (g, s + 1 if s % 2 else s - 1)
            pairs.append((g * strips + s, to[0] * strips + to[1]))
    return pairs


def tile(c):
    return pl.ds(pl.multiple_of(c * LANES, LANES), LANES)


def call(kernel, out_shape, args, after=()):
    count = len(args)

    def body(*refs):
        kernel(*refs[:count], *refs[count + len(after) :])

    return pl.pallas_call(
        body,
        out_shape=out_shape,
        in_specs=[VMEM] * count + [pl.BlockSpec(memory_space=pl.ANY)] * len(after),
        out_specs=jax.tree.map(lambda _: VMEM, out_shape),
        cost_estimate=pl.CostEstimate(flops=2_000_000, bytes_accessed=2_000_000, transcendentals=0),
        compiler_params=pltpu.CompilerParams(vmem_limit_bytes=16 * 1024 * 1024),
    )(*args, *after)


def array(*shape):
    return jax.ShapeDtypeStruct(shape, jnp.float32)


def load_kernel(order, *refs):
    density, materials, flags, tf_color, tf_opacity = refs[:5]
    brick, held_materials, held_color, held_opacity, layer, inner_y, outer_y, held_flags, sems = refs[5:]
    slices, rows, columns = density.shape
    pairs = (
        (density, brick.at[:, :, pl.ds(0, columns)]),
        (materials, held_materials),
        (flags, held_flags),
        (tf_color, held_color),
        (tf_opacity, held_opacity),
    )
    copies = [pltpu.make_async_copy(x, y, sems.at[i]) for i, (x, y) in enumerate(pairs)]
    for copy in copies[1:] + copies[:1]:
        copy.start()
    odd_z = lax.axis_index("depth") % 2
    odd_y = lax.axis_index("strip") % 2 == 1
    for copy in copies[1:]:
        copy.wait()
    half = columns // LANES // 2
    for i in range(half):
        given = held_materials[:, :, tile(order(1, i))].astype(jnp.float32)
        brick[:, :, columns + i * LANES : columns + (i + 1) * LANES] = given
    occupied = [held_flags[:, :].astype(jnp.float32)] * (LANES // flags.shape[1])
    occupied = jnp.concatenate(occupied, axis=1)
    brick[0, :ROWS, columns + half * LANES :] = jnp.broadcast_to(occupied, (ROWS, LANES))
    copies[0].wait()
    layer[0] = brick[(slices - 1) * odd_z, :, :columns]
    for z in range(slices):
        first, last = brick[z, :1, :columns], brick[z, rows - 1 :, :columns]
        inner_y[z : z + 1, :] = jnp.where(odd_y, first, last)
        outer_y[z : z + 1, :] = jnp.where(odd_y, last, first)


def by_lane(table):
    here = [table[m : m + 1, :] for m in range(table.shape[0])]
    last = table.shape[1] - 1
    further = [jnp.concatenate([t[:, 1:], t[:, last:]], axis=1) for t in here]
    return jnp.concatenate(here + here, axis=1), jnp.concatenate(further + further, axis=1)


def lookup_kernel(order, columns, start, brick, tf_color, tf_opacity, *refs):
    materials, out = refs if len(refs) == 2 else (None, refs[0])
    slices, rows = brick.shape[:2]
    knots = tf_opacity.shape[1]
    lane = lax.broadcasted_iota(jnp.int32, (1, LANES), 1)
    table = []
    for ch in range(3):
        value, further = by_lane(tf_color[ch])
        low = (further * 65535.0 + 0.5).astype(jnp.int32)
        high = jnp.floor((value * (32767.0 * 65536.0) - low.astype(jnp.float32)) * (1.0 / 65536.0) + 0.5)
        table.append(jnp.broadcast_to(high.astype(jnp.int32) * 65536 + low, (ROWS, LANES)))
    value, further = by_lane(tf_opacity[...])
    rates = jnp.broadcast_to(jnp.where(lane < LANES // 2, value, further - value), (ROWS, LANES))

    occupied = brick[0, :ROWS, columns + columns // 2 :]

    def look(t, index):
        return jnp.take_along_axis(t, index, axis=1, mode="promise_in_bounds")

    def body(at, _):
        i = start + at
        c = order(0, i)
        here = tile(c)
        present = look(occupied, jnp.full((ROWS, LANES), c, jnp.int32))
        for b in range(rows // ROWS):
            band = slice(b * ROWS, (b + 1) * ROWS)
            transmit = None
            for z in range(slices):
                position = jnp.clip(
                    (brick[z, band, here] + 3.0) * ((knots - 1) / 6.0), 0.0, knots - 1.0
                )
                whole = position.astype(jnp.int32)
                part = position - whole.astype(jnp.float32)
                if materials is None:
                    material = brick[z, band, tile(columns // LANES + i)].astype(jnp.int32)
                else:
                    material = materials[z, band, here]
                index = material * knots + whole
                rate = look(rates, index) + part * look(rates, index + LANES // 2)
                clear = jnp.exp(-(rate * present))
                weight = 1.0 - clear
                if z:
                    weight = weight * transmit
                of_low = (part * weight) * (1.0 / 65535.0)
                of_high = (weight - part * weight) * (1.0 / (32767.0 * 65536.0))
                for ch in range(3):
                    both = look(table[ch], index)
                    low = (both & 65535).astype(jnp.float32)
                    out[at, z * 3 + ch, band, :] = both.astype(jnp.float32) * of_high + low * of_low
                transmit = transmit * clear if z else clear
            out[at, slices * 3, band, :] = transmit
        return 0

    lax.fori_loop(0, out.shape[0], body, 0, unroll=out.shape[0])


def over(swap, nearer, farther):
    first = [jnp.where(swap, f, n) for n, f in zip(nearer, farther)]
    second = [jnp.where(swap, n, f) for n, f in zip(nearer, farther)]
    return [first[ch] + first[3] * second[ch] for ch in range(3)] + [first[3] * second[3]]


def hand_kernel(order, start, far_z, near_y, far_y, out):
    _, rows, _ = far_z.shape
    slices = near_y.shape[0]
    for i in range(out.shape[0]):
        here = tile(order(1, start + i))
        out[i, :rows, :] = far_z[0, :, here]
        out[i, rows : rows + slices, :] = near_y[:, here]
        out[i, rows + slices :, :] = far_y[:, here]


def column_step(brick, columns, c, z, band, v):
    tiles = columns // LANES
    lane = lax.broadcasted_iota(jnp.int32, (ROWS, LANES), 1)
    vl = brick[z, band, tile(jnp.maximum(c - 1, 0))] * jnp.where(c > 0, 1.0, 0.0)
    vr = brick[z, band, tile(jnp.minimum(c + 1, tiles - 1))] * jnp.where(c < tiles - 1, 1.0, 0.0)
    return pltpu.roll(jnp.where(lane == 0, vr, v), LANES - 1, 1) - pltpu.roll(
        jnp.where(lane == LANES - 1, vl, v), 1, 1
    )


def steps_kernel(order, columns, start, brick, out):
    slices, rows = brick.shape[:2]
    for i in range(out.shape[0]):
        c = order(0, start + i)
        for z in range(slices):
            for b in range(rows // ROWS):
                band = slice(b * ROWS, (b + 1) * ROWS)
                out[i, z, band, :] = column_step(brick, columns, c, z, band, brick[z, band, tile(c)])


def shade(order, columns, start, outs, brick, beside, weights, layer, near_row, far_row, across, odd_slab, finish):
    slices, rows = brick.shape[:2]
    bands = rows // ROWS
    row = lax.broadcasted_iota(jnp.int32, (ROWS, LANES), 0)
    chip, chips = lax.axis_index("depth") // 2, lax.axis_size("depth") // 2
    at_y = lax.axis_index("strip")
    odd_y = at_y % 2 == 1
    has_nearer = jnp.where(chip > 0, 1.0, 0.0)
    has_farther = jnp.where(chip < chips - 1, 1.0, 0.0)
    has_top = jnp.where(at_y > 0, 1.0, 0.0)
    has_bottom = jnp.where(at_y < lax.axis_size("strip") - 1, 1.0, 0.0)
    facing_layer = jnp.where(odd_slab, slices - 1, 0)
    work = [(out, h) for out in outs for h in range(out.shape[0])]
    for i, (out, h) in enumerate(work, start):
        c = order(0, i)
        here = tile(c)
        d = [[brick[z, b * ROWS : (b + 1) * ROWS, here] for b in range(bands)] for z in range(slices)]
        for b in range(bands):
            band = slice(b * ROWS, (b + 1) * ROWS)
            radiance = [None] * 3
            for z in range(slices):
                v = d[z][b]
                if z == 0:
                    nearer = jnp.where(odd_slab, beside[facing_layer, band, here], layer(i, c, band) * has_nearer)
                else:
                    nearer = d[z - 1][b]
                if z == slices - 1:
                    farther = jnp.where(odd_slab, layer(i, c, band) * has_farther, beside[facing_layer, band, here])
                else:
                    farther = d[z + 1][b]
                dz = farther - nearer
                if b == 0:
                    top = jnp.where(odd_y, near_row(i, c, z), far_row(i, c, z))
                    top = jnp.broadcast_to(top * has_top, (ROWS, LANES))
                else:
                    top = d[z][b - 1]
                if b == bands - 1:
                    bottom = jnp.where(odd_y, far_row(i, c, z), near_row(i, c, z))
                    bottom = jnp.broadcast_to(bottom * has_bottom, (ROWS, LANES))
                else:
                    bottom = d[z][b + 1]
                dy = pltpu.roll(jnp.where(row == 0, bottom, v), ROWS - 1, 0) - pltpu.roll(
                    jnp.where(row == ROWS - 1, top, v), 1, 0
                )
                dx = across(i, c, z, band, v)
                facing = jnp.abs(dx + 2.0 * (dy + dz))
                lighting = ambient + (diffuse / 3.0) * facing * lax.rsqrt(
                    4.0 + (dx * dx + dy * dy + dz * dz)
                )
                for ch in range(3):
                    term = weights[i - start, z * 3 + ch, band, :] * lighting
                    radiance[ch] = radiance[ch] + term if z else term
            image = finish(i - start, band, radiance + [weights[i - start, slices * 3, band, :]])
            for ch in range(4):
                out[h, ch, band, :] = image[ch]


def own_kernel(order, columns, start, brick, beside, weights, far_z, near_y, far_y, out):
    shade(
        order,
        columns,
        start,
        [out],
        brick,
        beside,
        weights,
        lambda i, c, band: far_z[0, band, tile(c)],
        lambda i, c, z: near_y[z : z + 1, tile(c)],
        lambda i, c, z: far_y[z : z + 1, tile(c)],
        lambda i, c, z, band, v: column_step(brick, columns, c, z, band, v),
        lax.axis_index("depth") % 2 == 1,
        lambda i, band, image: image,
    )


def chip_kernel(order, columns, start, brick, beside, weights, steps, handed, mine, *outs):
    slices, rows = brick.shape[:2]
    odd = lax.axis_index("depth") % 2 == 1
    shade(
        order,
        columns,
        start,
        outs,
        brick,
        beside,
        weights,
        lambda i, c, band: handed[i - start, band, :],
        lambda i, c, z: handed[i - start, rows + z : rows + z + 1, :],
        lambda i, c, z: handed[i - start, rows + slices + z : rows + slices + z + 1, :],
        lambda i, c, z, band, v: steps[i - start, z, band, :],
        lax.axis_index("depth") % 2 == 0,
        lambda i, band, image: over(odd, [mine[i, ch, band, :] for ch in range(4)], image),
    )


def chip_order(chips):
    return sorted(range(chips), key=lambda k: (-k.bit_count(), k))


def finish_kernel(*refs):
    given, out = dict(zip(chip_order(len(refs) - 1), refs)), refs[-1]
    pieces = [given[k] for k in range(len(given))]
    chip = lax.axis_index("depth") // 2
    for h in range(pieces[0].shape[0]):
        values = [[piece[h, ch] for ch in range(4)] for piece in pieces]
        bit = 0
        while len(values) > 1:
            swap = (chip >> bit) % 2 == 1
            values = [over(swap, values[k], values[k + 1]) for k in range(0, len(values), 2)]
            bit += 1
        here = slice(h * LANES, (h + 1) * LANES)
        for ch in range(3):
            out[ch, :, here] = values[0][ch]
        out[3, :, here] = 1.0 - values[0][3]


def composite_over(nearer, farther):
    return jnp.concatenate(
        [nearer[:, :3] + nearer[:, 3:] * farther[:, :3], nearer[:, 3:] * farther[:, 3:]], axis=1
    )


def on_device(density, materials, occupancy_flags, tf_color, tf_opacity):
    slices, rows, columns = density.shape
    tiles = columns // LANES
    groups, strips = lax.axis_size("depth"), lax.axis_size("strip")
    width = columns // groups
    chips, half = groups // 2, tiles // 2
    paired = chips & (chips - 1) == 0 and width % LANES == 0
    per = width // LANES if paired else half
    ks = chip_order(chips) if paired else [0]

    def order(other, i):
        index = lax.axis_index("depth")
        parity = (index + other) % 2
        if not paired:
            return parity * half + i
        k = sum(jnp.where(i // per == n, ks[n], 0) for n in range(chips))
        return ((index // 2 ^ k) * 2 + parity) * per + i % per

    given = (density, materials, occupancy_flags[0], tf_color.transpose(1, 0, 2), tf_opacity)
    whole = array(slices, rows, columns + half * LANES + LANES)
    edge = array(slices, columns)
    brick, materials, tf_color, tf_opacity, layer, inner_y, outer_y = pl.pallas_call(
        functools.partial(load_kernel, order),
        out_shape=[whole]
        + [jax.ShapeDtypeStruct(given[n].shape, given[n].dtype) for n in (1, 3, 4)]
        + [array(1, rows, columns), edge, edge],
        in_specs=[pl.BlockSpec(memory_space=pltpu.HBM)] * 5,
        out_specs=[VMEM] * 7,
        scratch_shapes=[pltpu.VMEM(given[2].shape, jnp.int32), pltpu.SemaphoreType.DMA((5,))],
        compiler_params=pltpu.CompilerParams(vmem_limit_bytes=16 * 1024 * 1024),
    )(*[pltpu.with_memory_space_constraint(x, pltpu.HBM) for x in given])
    both = ("depth", "strip")
    beside = lax.ppermute(brick, "depth", inner_pairs(groups))
    far_z = lax.ppermute(layer, both, outer_pairs(groups, strips, "depth"))
    near_y = lax.ppermute(inner_y, "strip", inner_pairs(strips))
    far_y = lax.ppermute(outer_y, both, outer_pairs(groups, strips, "strip"))

    far = (chips - 1) * per if paired else half

    def weigh(first, count, after=()):
        lookup = functools.partial(lookup_kernel, order, columns, first)
        shape = array(count, slices * 3 + 1, rows, LANES)
        mine = call(lookup, shape, (brick, tf_color, tf_opacity, materials), after)
        return mine, call(lookup, shape, (beside, tf_color, tf_opacity), (mine,))

    weights, weights_beside = weigh(0, far)
    def hand(first, count, after):
        handing = call(
            functools.partial(hand_kernel, order, first),
            array(count, rows + 2 * slices, LANES),
            (far_z, near_y, far_y),
            after,
        )
        return lax.ppermute(handing, "depth", inner_pairs(groups))

    handed = hand(0, far, (weights_beside,))

    def images(first, count, blocks, handed, weights, weights_beside):
        steps = call(
            functools.partial(steps_kernel, order, columns, first),
            array(count, slices, rows, LANES),
            (beside,),
            (weights_beside,),
        )
        mine = call(
            functools.partial(own_kernel, order, columns, first),
            array(count, 4, rows, LANES),
            (brick, beside, weights, far_z, near_y, far_y),
        )
        return call(
            functools.partial(chip_kernel, order, columns, first),
            [array(count // blocks, 4, rows, LANES)] * blocks,
            (beside, brick, weights_beside, steps, handed, mine),
        )

    if paired:
        sent = images(0, far, chips - 1, handed, weights, weights_beside)
        moved = [
            lax.ppermute(image, "depth", [(i, i ^ (2 * k)) for i in range(groups)])
            for image, k in zip(sent, ks)
        ]
        late = sent[-1:]
        (kept,) = images(far, per, 1, hand(far, per, late), *weigh(far, per, late))
        return call(finish_kernel, array(4, rows, width), (*moved, kept))

    (image,) = images(0, half, 1, handed, weights, weights_beside)
    clear = jnp.zeros_like(image).at[:, 3].set(1.0)
    odd = lax.axis_index("depth") % 2 == 1
    partial_value = jnp.concatenate(
        [jnp.where(odd, clear, image), jnp.where(odd, image, clear)], axis=0
    )
    natural = partial_value.transpose(1, 2, 0, 3).reshape(4, rows, groups, width)
    pieces = lax.all_to_all(
        natural.transpose(2, 0, 1, 3), "depth", split_axis=0, concat_axis=0, tiled=True
    )
    while pieces.shape[0] > 1:
        pieces = composite_over(pieces[0::2], pieces[1::2])
    finished = pieces[0]
    return jnp.concatenate([finished[:3], 1.0 - finished[3:]], axis=0)


def solution(mesh):
    placed = (
        P("depth", "strip", None),
        P("depth", "strip", None),
        P("depth", "strip", None),
        P(),
        P(),
    )
    return jax.shard_map(
        on_device, mesh=mesh, in_specs=placed, out_specs=P(None, "strip", "depth"), check_vma=False
    )
```

```python
import functools

import jax
import jax.numpy as jnp
from jax import lax
from jax.experimental import pallas as pl
from jax.experimental.pallas import tpu as pltpu
from jax.sharding import PartitionSpec as P

ambient = 0.3
diffuse = 0.7
LANES = 128
ROWS = 8
VMEM = pl.BlockSpec(memory_space=pltpu.VMEM)


def inner_pairs(count):
    return [(i, i ^ 1) for i in range(count)]


def outer_pairs(groups, strips, axis):
    pairs = []
    for g in range(groups):
        for s in range(strips):
            if axis == "depth":
                to = (g, s ^ 1) if g in (0, groups - 1) else (g + 1 if g % 2 else g - 1, s)
            else:
                to = (g ^ 1, s) if s in (0, strips - 1) else (g, s + 1 if s % 2 else s - 1)
            pairs.append((g * strips + s, to[0] * strips + to[1]))
    return pairs


def tile(c):
    return pl.ds(pl.multiple_of(c * LANES, LANES), LANES)


def call(kernel, out_shape, args, after=()):
    count = len(args)

    def body(*refs):
        kernel(*refs[:count], *refs[count + len(after) :])

    return pl.pallas_call(
        body,
        out_shape=out_shape,
        in_specs=[VMEM] * count + [pl.BlockSpec(memory_space=pl.ANY)] * len(after),
        out_specs=jax.tree.map(lambda _: VMEM, out_shape),
        cost_estimate=pl.CostEstimate(flops=2_000_000, bytes_accessed=2_000_000, transcendentals=0),
        compiler_params=pltpu.CompilerParams(vmem_limit_bytes=16 * 1024 * 1024),
    )(*args, *after)


def array(*shape):
    return jax.ShapeDtypeStruct(shape, jnp.float32)


def load_kernel(order, *refs):
    density, materials, flags, tf_color, tf_opacity = refs[:5]
    brick, held_materials, held_color, held_opacity, layer, inner_y, outer_y, held_flags, sems = refs[5:]
    slices, rows, columns = density.shape
    pairs = (
        (density, brick.at[:, :, pl.ds(0, columns)]),
        (materials, held_materials),
        (flags, held_flags),
        (tf_color, held_color),
        (tf_opacity, held_opacity),
    )
    copies = [pltpu.make_async_copy(x, y, sems.at[i]) for i, (x, y) in enumerate(pairs)]
    for copy in copies[1:] + copies[:1]:
        copy.start()
    odd_z = lax.axis_index("depth") % 2
    odd_y = lax.axis_index("strip") % 2 == 1
    for copy in copies[1:]:
        copy.wait()
    half = columns // LANES // 2
    for i in range(half):
        given = held_materials[:, :, tile(order(1, i))].astype(jnp.float32)
        brick[:, :, columns + i * LANES : columns + (i + 1) * LANES] = given
    occupied = [held_flags[:, :].astype(jnp.float32)] * (LANES // flags.shape[1])
    occupied = jnp.concatenate(occupied, axis=1)
    brick[0, :ROWS, columns + half * LANES :] = jnp.broadcast_to(occupied, (ROWS, LANES))
    copies[0].wait()
    layer[0] = brick[(slices - 1) * odd_z, :, :columns]
    for z in range(slices):
        first, last = brick[z, :1, :columns], brick[z, rows - 1 :, :columns]
        inner_y[z : z + 1, :] = jnp.where(odd_y, first, last)
        outer_y[z : z + 1, :] = jnp.where(odd_y, last, first)


def by_lane(table):
    here = [table[m : m + 1, :] for m in range(table.shape[0])]
    last = table.shape[1] - 1
    further = [jnp.concatenate([t[:, 1:], t[:, last:]], axis=1) for t in here]
    return jnp.concatenate(here + here, axis=1), jnp.concatenate(further + further, axis=1)


def lookup_kernel(order, columns, start, brick, tf_color, tf_opacity, *refs):
    materials, out = refs if len(refs) == 2 else (None, refs[0])
    slices, rows = brick.shape[:2]
    knots = tf_opacity.shape[1]
    lane = lax.broadcasted_iota(jnp.int32, (1, LANES), 1)
    table = []
    for ch in range(3):
        value, further = by_lane(tf_color[ch])
        low = (further * 65535.0 + 0.5).astype(jnp.int32)
        high = jnp.floor((value * (32767.0 * 65536.0) - low.astype(jnp.float32)) * (1.0 / 65536.0) + 0.5)
        table.append(jnp.broadcast_to(high.astype(jnp.int32) * 65536 + low, (ROWS, LANES)))
    value, further = by_lane(tf_opacity[...])
    rates = jnp.broadcast_to(jnp.where(lane < LANES // 2, value, further - value), (ROWS, LANES))

    occupied = brick[0, :ROWS, columns + columns // 2 :]

    def look(t, index):
        return jnp.take_along_axis(t, index, axis=1, mode="promise_in_bounds")

    def body(at, _):
        i = start + at
        c = order(0, i)
        here = tile(c)
        present = look(occupied, jnp.full((ROWS, LANES), c, jnp.int32))
        for b in range(rows // ROWS):
            band = slice(b * ROWS, (b + 1) * ROWS)
            transmit = None
            for z in range(slices):
                position = jnp.clip(
                    (brick[z, band, here] + 3.0) * ((knots - 1) / 6.0), 0.0, knots - 1.0
                )
                whole = position.astype(jnp.int32)
                part = position - whole.astype(jnp.float32)
                if materials is None:
                    material = brick[z, band, tile(columns // LANES + i)].astype(jnp.int32)
                else:
                    material = materials[z, band, here]
                index = material * knots + whole
                rate = look(rates, index) + part * look(rates, index + LANES // 2)
                clear = jnp.exp(-(rate * present))
                weight = 1.0 - clear
                if z:
                    weight = weight * transmit
                of_low = (part * weight) * (1.0 / 65535.0)
                of_high = (weight - part * weight) * (1.0 / (32767.0 * 65536.0))
                for ch in range(3):
                    both = look(table[ch], index)
                    low = (both & 65535).astype(jnp.float32)
                    out[at, z * 3 + ch, band, :] = both.astype(jnp.float32) * of_high + low * of_low
                transmit = transmit * clear if z else clear
            out[at, slices * 3, band, :] = transmit
        return 0

    lax.fori_loop(0, out.shape[0], body, 0, unroll=out.shape[0])


def over(swap, nearer, farther):
    first = [jnp.where(swap, f, n) for n, f in zip(nearer, farther)]
    second = [jnp.where(swap, n, f) for n, f in zip(nearer, farther)]
    return [first[ch] + first[3] * second[ch] for ch in range(3)] + [first[3] * second[3]]


def hand_kernel(order, start, far_z, near_y, far_y, out):
    _, rows, _ = far_z.shape
    slices = near_y.shape[0]
    for i in range(out.shape[0]):
        here = tile(order(1, start + i))
        out[i, :rows, :] = far_z[0, :, here]
        out[i, rows : rows + slices, :] = near_y[:, here]
        out[i, rows + slices :, :] = far_y[:, here]


def column_step(brick, columns, c, z, band, v):
    tiles = columns // LANES
    lane = lax.broadcasted_iota(jnp.int32, (ROWS, LANES), 1)
    vl = brick[z, band, tile(jnp.maximum(c - 1, 0))] * jnp.where(c > 0, 1.0, 0.0)
    vr = brick[z, band, tile(jnp.minimum(c + 1, tiles - 1))] * jnp.where(c < tiles - 1, 1.0, 0.0)
    return pltpu.roll(jnp.where(lane == 0, vr, v), LANES - 1, 1) - pltpu.roll(
        jnp.where(lane == LANES - 1, vl, v), 1, 1
    )


def steps_kernel(order, columns, start, brick, out):
    slices, rows = brick.shape[:2]
    for i in range(out.shape[0]):
        c = order(0, start + i)
        for z in range(slices):
            for b in range(rows // ROWS):
                band = slice(b * ROWS, (b + 1) * ROWS)
                out[i, z, band, :] = column_step(brick, columns, c, z, band, brick[z, band, tile(c)])


def shade(order, columns, start, outs, brick, beside, weights, layer, near_row, far_row, across, odd_slab, finish):
    slices, rows = brick.shape[:2]
    bands = rows // ROWS
    row = lax.broadcasted_iota(jnp.int32, (ROWS, LANES), 0)
    chip, chips = lax.axis_index("depth") // 2, lax.axis_size("depth") // 2
    at_y = lax.axis_index("strip")
    odd_y = at_y % 2 == 1
    has_nearer = jnp.where(chip > 0, 1.0, 0.0)
    has_farther = jnp.where(chip < chips - 1, 1.0, 0.0)
    has_top = jnp.where(at_y > 0, 1.0, 0.0)
    has_bottom = jnp.where(at_y < lax.axis_size("strip") - 1, 1.0, 0.0)
    facing_layer = jnp.where(odd_slab, slices - 1, 0)
    work = [(out, h) for out in outs for h in range(out.shape[0])]
    for i, (out, h) in enumerate(work, start):
        c = order(0, i)
        here = tile(c)
        d = [[brick[z, b * ROWS : (b + 1) * ROWS, here] for b in range(bands)] for z in range(slices)]
        for b in range(bands):
            band = slice(b * ROWS, (b + 1) * ROWS)
            radiance = [None] * 3
            for z in range(slices):
                v = d[z][b]
                if z == 0:
                    nearer = jnp.where(odd_slab, beside[facing_layer, band, here], layer(i, c, band) * has_nearer)
                else:
                    nearer = d[z - 1][b]
                if z == slices - 1:
                    farther = jnp.where(odd_slab, layer(i, c, band) * has_farther, beside[facing_layer, band, here])
                else:
                    farther = d[z + 1][b]
                dz = farther - nearer
                if b == 0:
                    top = jnp.where(odd_y, near_row(i, c, z), far_row(i, c, z))
                    top = jnp.broadcast_to(top * has_top, (ROWS, LANES))
                else:
                    top = d[z][b - 1]
                if b == bands - 1:
                    bottom = jnp.where(odd_y, far_row(i, c, z), near_row(i, c, z))
                    bottom = jnp.broadcast_to(bottom * has_bottom, (ROWS, LANES))
                else:
                    bottom = d[z][b + 1]
                dy = pltpu.roll(jnp.where(row == 0, bottom, v), ROWS - 1, 0) - pltpu.roll(
                    jnp.where(row == ROWS - 1, top, v), 1, 0
                )
                dx = across(i, c, z, band, v)
                facing = jnp.abs(dx + 2.0 * (dy + dz))
                lighting = ambient + (diffuse / 3.0) * facing * lax.rsqrt(
                    4.0 + (dx * dx + dy * dy + dz * dz)
                )
                for ch in range(3):
                    term = weights[i - start, z * 3 + ch, band, :] * lighting
                    radiance[ch] = radiance[ch] + term if z else term
            image = finish(i - start, band, radiance + [weights[i - start, slices * 3, band, :]])
            for ch in range(4):
                out[h, ch, band, :] = image[ch]


def own_kernel(order, columns, start, brick, beside, weights, far_z, near_y, far_y, out):
    shade(
        order,
        columns,
        start,
        [out],
        brick,
        beside,
        weights,
        lambda i, c, band: far_z[0, band, tile(c)],
        lambda i, c, z: near_y[z : z + 1, tile(c)],
        lambda i, c, z: far_y[z : z + 1, tile(c)],
        lambda i, c, z, band, v: column_step(brick, columns, c, z, band, v),
        lax.axis_index("depth") % 2 == 1,
        lambda i, band, image: image,
    )


def chip_kernel(order, columns, start, brick, beside, weights, steps, handed, mine, *outs):
    slices, rows = brick.shape[:2]
    odd = lax.axis_index("depth") % 2 == 1
    shade(
        order,
        columns,
        start,
        outs,
        brick,
        beside,
        weights,
        lambda i, c, band: handed[i - start, band, :],
        lambda i, c, z: handed[i - start, rows + z : rows + z + 1, :],
        lambda i, c, z: handed[i - start, rows + slices + z : rows + slices + z + 1, :],
        lambda i, c, z, band, v: steps[i - start, z, band, :],
        lax.axis_index("depth") % 2 == 0,
        lambda i, band, image: over(odd, [mine[i, ch, band, :] for ch in range(4)], image),
    )


def chip_order(chips):
    return sorted(range(chips), key=lambda k: (-k.bit_count(), k))


def finish_kernel(*refs):
    given, out = dict(zip(chip_order(len(refs) - 1), refs)), refs[-1]
    pieces = [given[k] for k in range(len(given))]
    chip = lax.axis_index("depth") // 2
    for h in range(pieces[0].shape[0]):
        values = [[piece[h, ch] for ch in range(4)] for piece in pieces]
        if len(values) == 4:
            turned = lax.axis_index("strip") > 0
            one, two = values[1], values[2]
            values[1] = [jnp.where(turned, y, x) for x, y in zip(one, two)]
            values[2] = [jnp.where(turned, x, y) for x, y in zip(one, two)]
        bit = 0
        while len(values) > 1:
            swap = (chip >> bit) % 2 == 1
            values = [over(swap, values[k], values[k + 1]) for k in range(0, len(values), 2)]
            bit += 1
        here = slice(h * LANES, (h + 1) * LANES)
        for ch in range(3):
            out[ch, :, here] = values[0][ch]
        out[3, :, here] = 1.0 - values[0][3]


def composite_over(nearer, farther):
    return jnp.concatenate(
        [nearer[:, :3] + nearer[:, 3:] * farther[:, :3], nearer[:, 3:] * farther[:, 3:]], axis=1
    )


def on_device(density, materials, occupancy_flags, tf_color, tf_opacity):
    slices, rows, columns = density.shape
    tiles = columns // LANES
    groups, strips = lax.axis_size("depth"), lax.axis_size("strip")
    width = columns // groups
    chips, half = groups // 2, tiles // 2
    paired = chips & (chips - 1) == 0 and width % LANES == 0
    per = width // LANES if paired else half
    ks = chip_order(chips) if paired else [0]

    def order(other, i):
        index = lax.axis_index("depth")
        parity = (index + other) % 2
        if not paired:
            return parity * half + i
        k = sum(jnp.where(i // per == n, ks[n], 0) for n in range(chips))
        k = jnp.where((lax.axis_index("strip") > 0) & (k > 0) & (k < 3) & (chips == 4), 3 - k, k)
        return ((index // 2 ^ k) * 2 + parity) * per + i % per

    given = (density, materials, occupancy_flags[0], tf_color.transpose(1, 0, 2), tf_opacity)
    whole = array(slices, rows, columns + half * LANES + LANES)
    edge = array(slices, columns)
    brick, materials, tf_color, tf_opacity, layer, inner_y, outer_y = pl.pallas_call(
        functools.partial(load_kernel, order),
        out_shape=[whole]
        + [jax.ShapeDtypeStruct(given[n].shape, given[n].dtype) for n in (1, 3, 4)]
        + [array(1, rows, columns), edge, edge],
        in_specs=[pl.BlockSpec(memory_space=pltpu.HBM)] * 5,
        out_specs=[VMEM] * 7,
        scratch_shapes=[pltpu.VMEM(given[2].shape, jnp.int32), pltpu.SemaphoreType.DMA((5,))],
        compiler_params=pltpu.CompilerParams(vmem_limit_bytes=16 * 1024 * 1024),
    )(*[pltpu.with_memory_space_constraint(x, pltpu.HBM) for x in given])
    both = ("depth", "strip")
    beside = lax.ppermute(brick, "depth", inner_pairs(groups))
    far_z = lax.ppermute(layer, both, outer_pairs(groups, strips, "depth"))
    near_y = lax.ppermute(inner_y, "strip", inner_pairs(strips))
    far_y = lax.ppermute(outer_y, both, outer_pairs(groups, strips, "strip"))

    far = (chips - 1) * per if paired else half

    def weigh(first, count, after=()):
        lookup = functools.partial(lookup_kernel, order, columns, first)
        shape = array(count, slices * 3 + 1, rows, LANES)
        mine = call(lookup, shape, (brick, tf_color, tf_opacity, materials), after)
        return mine, call(lookup, shape, (beside, tf_color, tf_opacity), (mine,))

    weights, weights_beside = weigh(0, far)
    def hand(first, count, after):
        handing = call(
            functools.partial(hand_kernel, order, first),
            array(count, rows + 2 * slices, LANES),
            (far_z, near_y, far_y),
            after,
        )
        return lax.ppermute(handing, "depth", inner_pairs(groups))

    handed = hand(0, far, (weights_beside,))

    def images(first, count, blocks, handed, weights, weights_beside):
        steps = call(
            functools.partial(steps_kernel, order, columns, first),
            array(count, slices, rows, LANES),
            (beside,),
            (weights_beside,),
        )
        mine = call(
            functools.partial(own_kernel, order, columns, first),
            array(count, 4, rows, LANES),
            (brick, beside, weights, far_z, near_y, far_y),
        )
        return call(
            functools.partial(chip_kernel, order, columns, first),
            [array(count // blocks, 4, rows, LANES)] * blocks,
            (beside, brick, weights_beside, steps, handed, mine),
        )

    if paired:
        sent = images(0, far, chips - 1, handed, weights, weights_beside)
        moved = [
            lax.ppermute(image, both, [
                (g * strips + t, (g ^ 2 * (3 - k if t and k < 3 and chips == 4 else k)) * strips + t)
                for g in range(groups) for t in range(strips)
            ])
            for image, k in zip(sent, ks)
        ]
        late = sent[-1:]
        (kept,) = images(far, per, 1, hand(far, per, late), *weigh(far, per, late))
        return call(finish_kernel, array(4, rows, width), (*moved, kept))

    (image,) = images(0, half, 1, handed, weights, weights_beside)
    clear = jnp.zeros_like(image).at[:, 3].set(1.0)
    odd = lax.axis_index("depth") % 2 == 1
    partial_value = jnp.concatenate(
        [jnp.where(odd, clear, image), jnp.where(odd, image, clear)], axis=0
    )
    natural = partial_value.transpose(1, 2, 0, 3).reshape(4, rows, groups, width)
    pieces = lax.all_to_all(
        natural.transpose(2, 0, 1, 3), "depth", split_axis=0, concat_axis=0, tiled=True
    )
    while pieces.shape[0] > 1:
        pieces = composite_over(pieces[0::2], pieces[1::2])
    finished = pieces[0]
    return jnp.concatenate([finished[:3], 1.0 - finished[3:]], axis=0)


def solution(mesh):
    placed = (
        P("depth", "strip", None),
        P("depth", "strip", None),
        P("depth", "strip", None),
        P(),
        P(),
    )
    return jax.shard_map(
        on_device, mesh=mesh, in_specs=placed, out_specs=P(None, "strip", "depth"), check_vma=False
    )
```
